256 devices in a mesh: gx: 16 (over x, y), gy: 8 (over z), gz: 2 (over core).
Axes of the slice: x: 4, y: 4, z: 8, core: 2. Of those that a mesh axis runs over, the one named last changes fastest.
Arguments:
- charges: float32 [2, 128, 128, 16], P('gz', ('gx', 'gy')), may hold values from -6 to 6
- heights: float32 [2, 128, 128, 16], P('gz', ('gx', 'gy')), may hold values from 0 to 255
- columns: int32 [2, 128, 128, 16], P('gz', ('gx', 'gy')), may hold values from 0 to 511
- counts: int32 [2, 128, 128], P('gz', ('gx', 'gy')), may hold values from 1 to 16, 1024 in all within a row
- bands: float32 [2, 5], replicated, may hold values from 0.1 to 1
- cycle_kernel: float32 [64], replicated, may hold values from 0.5 to 4
Outputs:
- grid_potential: float32 [256, 256, 512], P('gx', 'gy', 'gz')
- atom_potential: float32 [2, 128, 128, 16], P('gz', ('gx', 'gy'))
The draws below stay inside these ranges and needn't reach their ends.
Inputs may be any that keep to these rules, and one draw needn't show every extreme that they name: `counts`: each device has live slots to every owner, and 1024 live slots in all.
All inputs are finite; a program needn't handle non-finite values.
Results may differ from the reference program's by a relative error of at most 0.0036.
Values sent between devices are 32-bit elements; how exact they have to be, the bound alone decides.
No kernel may reach another device: no remote copies, remote signals or barrier semaphores. Data moves between devices by JAX's collectives and lax.ppermute only.
A program may use at most 64 MiB of HBM per device.

```python
import math
import jax
import jax.numpy as jnp
import numpy as np
from jax import lax

CX = 16
CY = 32
CZ = 256
CAP = 16
LEVELS = 2
BANDS = 4
DEST = 128
COLS = 512
NX = 256
NY = 256
NZ = 512
XC = 64
N_GX = 16
N_GY = 8
N_GZ = 2


def with_ends(values, stream_key, least, largest):
    extent = values.shape
    spot = [jax.random.randint(jax.random.fold_in(stream_key, axis), (), 0, extent[axis]) for axis in range(len(extent))]
    values = values.at[tuple(spot)].set(least)
    longest = extent.index(max(extent))
    spot[longest] = (spot[longest] + 1) % extent[longest]
    return values.at[tuple(spot)].set(largest)


def levels(rng, dims, pieces, low, high):
    gain, own = 1.0, jax.random.fold_in(rng, 6)
    for dim, parts in pieces:
        draws = jnp.exp(jax.random.uniform(jax.random.fold_in(own, dim), (parts,), jnp.float32, low / len(pieces), high / len(pieces)))
        gain = gain * jnp.repeat(draws, dims[dim] // parts).reshape([-1 if axis == dim else 1 for axis in range(len(dims))])
    return gain


def profile(amount, total, bound, slope):
    weights = [(1 << 20) // math.isqrt(standing ** slope) + 1 for standing in range(2, amount + 1)]
    surplus, holding = total - bound - (amount - 1), [1] * (amount - 1)
    while surplus > 0:
        candidates = [i for i in range(amount - 1) if holding[i] < bound]
        whole, left = sum([weights[i] for i in candidates]), surplus
        for i in candidates:
            more = min(bound - holding[i], max(1, left * weights[i] // whole), surplus)
            holding[i] = holding[i] + more
            surplus = surplus - more
    return np.array([bound] + holding)


def ragged_sizes(key, count, total, reach, skew):
    if count == 2:
        one = jax.random.randint(key, (), max(1, total - reach), min(reach, total - 1) + 1)
        return jnp.stack([one, total - one])
    sizes = jnp.asarray(profile(count, total, reach, skew), jnp.int32)
    twos = (count - 1) // 2
    giver, sink = sizes[1:1 + 2 * twos:2], sizes[2:2 + 2 * twos:2]
    margin = jnp.minimum(giver - 1, reach - sink)
    moved = jax.random.randint(jax.random.fold_in(key, 1), (twos,), 0, 1 << 20) % (margin + 1)
    sizes = sizes.at[1:1 + 2 * twos:2].set(giver - moved).at[2:2 + 2 * twos:2].set(sink + moved)
    return sizes[jax.random.permutation(jax.random.fold_in(key, 2), count)]


def normal_values(stream_key, extent, width, most, cuts=(), held_as=jnp.bfloat16):
    loudness = levels(stream_key, extent, cuts, -0.22, 0.18) if cuts else 1.0
    result = jax.random.normal(stream_key, extent, jnp.float32) * width * loudness
    return jnp.minimum(jnp.maximum(result, -most), most).astype(held_as)


def setup_inputs(seed: int = 0) -> dict:
    streams_of = jax.random.split(jax.random.key(seed), 7)
    return {
        "charges": normal_values(streams_of[0], (N_GZ, DEST, DEST, CAP), 1.0, 6.0, ((0, 2), (1, 128)), jnp.float32),
        "heights": jnp.clip(255.0 * jax.random.uniform(streams_of[1], (N_GZ, DEST, DEST, CAP), jnp.float32) ** levels(streams_of[1], (N_GZ, DEST, DEST, CAP), ((0, 2), (1, 128)), -0.2, 0.2), 0.0, 255.0),
        "columns": with_ends(jax.random.randint(streams_of[2], (N_GZ, DEST, DEST, CAP), 0, COLS), jax.random.fold_in(streams_of[2], 1), 0, COLS - 1).astype(jnp.int32),
        "counts": jax.vmap(lambda own: ragged_sizes(own, DEST, DEST * CAP // 2, CAP, 2))(jax.random.split(streams_of[3], N_GZ * DEST)).reshape((N_GZ, DEST, DEST)).astype(jnp.int32),
        "bands": jnp.clip(jax.random.uniform(streams_of[4], (LEVELS, BANDS + 1), jnp.float32, 0.1, 1.0), 0.1, 1.0),
        "cycle_kernel": jnp.clip(jax.random.uniform(streams_of[5], (XC,), jnp.float32, 0.5, 4.0), 0.5, 4.0),
    }


def along(field, offset, axis):
    if axis < 2:
        return jnp.roll(field, -offset, axis)
    depth = field.shape[2]
    zeros = jnp.zeros(field.shape[:2] + (abs(offset),), field.dtype)
    if offset > 0:
        return jnp.concatenate([field[:, :, offset:], zeros], 2)
    return jnp.concatenate([zeros, field[:, :, :depth + offset]], 2)


def stencil(field, coeffs):
    total = coeffs[0] * field
    for axis in range(3):
        for offset in range(1, BANDS + 1):
            total = total + coeffs[offset] * (along(field, offset, axis) + along(field, -offset, axis))
    return total


def restrict(field):
    for axis in range(3):
        smooth = 0.25 * along(field, -1, axis) + 0.5 * field + 0.25 * along(field, 1, axis)
        field = lax.slice_in_dim(smooth, 0, smooth.shape[axis], 2, axis)
    return field


def prolong(coarse):
    for axis in range(3):
        upper = along(coarse, 1, axis)
        middle = 0.5 * (coarse + upper)
        shape = list(coarse.shape)
        shape[axis] = shape[axis] * 2
        coarse = jnp.stack([coarse, middle], axis + 1).reshape(shape)
    return coarse


def circulate(coarse, cycle_kernel):
    length = coarse.shape[0]
    rows = jnp.arange(length, dtype=jnp.int32)
    table = cycle_kernel[(rows[:, None] - rows[None, :]) % length]
    return jnp.einsum("ab,byz->ayz", table, coarse, precision=lax.Precision.HIGHEST)


def reference(charges, heights, columns, counts, bands, cycle_kernel):
    owners_all = N_GX * N_GY
    live = (jnp.arange(CAP, dtype=jnp.int32)[None, None, None, :] < counts[:, :, :, None]).astype(jnp.float32)

    def owners(array):
        return jnp.transpose(array, (0, 2, 1, 3)).reshape(N_GZ * owners_all, owners_all * CAP)

    masked = owners(charges * live)
    lifts = owners(heights)
    places = owners(columns)
    alive = owners(live)
    layers = jnp.arange(CZ, dtype=jnp.float32)

    def tent(height):
        return jnp.maximum(0.0, 1.0 - jnp.abs(layers[None, :] - height[:, None]))

    def spread_one(item):
        charge, height, place = item
        spread = (charge[:, None] * tent(height)).astype(jnp.bfloat16)
        spread = lax.optimization_barrier(spread).astype(jnp.float32)
        return jnp.zeros((CX * CY, CZ), jnp.float32).at[place].add(spread)

    blocks = lax.map(spread_one, (masked, lifts, places))
    field = blocks.reshape(N_GZ, N_GX, N_GY, CX, CY, CZ).transpose(1, 3, 2, 4, 0, 5).reshape(NX, NY, NZ)
    local_terms = []
    for level in range(LEVELS):
        local_terms.append(stencil(field, bands[level]))
        field = restrict(field)
    potential = circulate(field, cycle_kernel)
    for level in reversed(range(LEVELS)):
        potential = local_terms[level] + prolong(potential)
    rounded = potential.reshape(N_GX, CX, N_GY, CY, N_GZ, CZ).transpose(4, 0, 2, 1, 3, 5)
    rounded = rounded.reshape(N_GZ * owners_all, CX * CY, CZ).astype(jnp.bfloat16)

    def read_one(item):
        block, height, place, live_one = item
        rows = block[place].astype(jnp.float32)
        return jnp.sum(rows * tent(height), axis=1) * live_one

    at_atoms = lax.map(read_one, (rounded, lifts, places, alive)).reshape(N_GZ, owners_all, owners_all, CAP)
    return potential, at_atoms
```

```python
import jax
import jax.numpy as jnp
from jax import lax
from jax.experimental import pallas as pl
from jax.experimental.pallas import tpu as pltpu
from jax.sharding import PartitionSpec as P

CX, CY, CZ, CAP = 16, 32, 256, 16
BANDS = 4
SENDERS = 128
NEAR = 3 * CAP
FIELDS = 9 * NEAR
ROWS = 512
MSG = 640
F32, BF16 = jnp.float32, jnp.bfloat16
HIGH = lax.Precision.HIGHEST
VMEM_LIMIT = 48 * 1024 * 1024

OWN = 4
REACH = {
    (0, 0): (0, 9, 10, 0, 24),
    (-1, 0): (-4, 5, 6, 0, 24),
    (1, 0): (8, 5, 6, 0, 24),
    (0, -1): (0, 9, 9, -8, 16),
    (0, 1): (0, 9, 10, 16, 8),
    (-1, -1): (-4, 5, 5, -8, 16),
    (-1, 1): (-4, 5, 6, 16, 8),
    (1, -1): (8, 5, 5, -8, 16),
    (1, 1): (8, 5, 6, 16, 8),
}
FINE = {
    (0, 0): (0, 16, 0, 32),
    (-1, 0): (12, 4, 0, 32),
    (1, 0): (0, 4, 0, 32),
    (0, -1): (0, 16, 24, 8),
    (0, 1): (0, 16, 0, 8),
}


def iota(shape, dim):
    return lax.broadcasted_iota(jnp.int32, shape, dim)


def fiota(shape, dim):
    return iota(shape, dim).astype(F32)


def hat(distance, peak, slope):
    return jnp.maximum(0.0, peak - slope * jnp.abs(distance))


def mm(a, b):
    return lax.dot_general(a, b, (((1,), (0,)), ((), ())), preferred_element_type=F32)


def mm_nt(a, b):
    return lax.dot_general(a, b, (((1,), (1,)), ((), ())), preferred_element_type=F32)


def halves(a):
    top = a.astype(BF16)
    return top, (a - top.astype(F32)).astype(BF16)


def mm_exact_right(a, b):
    top, low = halves(a)
    return mm(top, b) + mm(low, b)


def mm_exact_left(a, b):
    top, low = halves(b)
    return mm(a, top) + mm(a, low)


def mm_both(a, b_top, b_low):
    top, low = halves(a)
    return mm(top, b_top) + (mm(low, b_top) + mm(top, b_low))


def block_index(dx, dy):
    return (dx + 1) * 3 + dy + 1


def atom_rows(table, block, first, count):
    base = block * NEAR + first
    return (
        table[pl.ds(base, count), :],
        table[pl.ds(base + CAP, count), :],
        table[pl.ds(base + 2 * CAP, count), :],
    )


def spread_chunk(charge, height, layer_ids):
    floor = jnp.floor(height)
    above = floor + 1.0
    low = charge * jnp.maximum(0.0, 1.0 - jnp.abs(floor - height))
    high = charge * jnp.maximum(0.0, 1.0 - jnp.abs(above - height))
    picked = jnp.where(layer_ids == floor, low, jnp.where(layer_ids == above, high, 0.0))
    return picked.astype(BF16)


def place_of(column):
    x = jnp.floor(column * (1.0 / CY))
    return x, column - CY * x


def tables_kernel(where_ref, bands_ref, cycle_ref, g0t, g0l, g1, g2t, g2l, l1, l2, cx, pz, rz):
    gx, gz = where_ref[0], where_ref[1]
    wide = CZ + 128
    shape = (CZ, wide)
    row = iota(shape, 0)
    lane = iota(shape, 1)
    first = CZ * gz
    out_layer = jnp.where(lane < CZ, first + lane, lane - (128 * gz))
    step = jnp.abs(first + row - out_layer)
    zero = jnp.zeros(shape, F32)
    total = jnp.where(step == 0, bands_ref[0, 0], zero)
    for k in range(1, BANDS + 1):
        total = jnp.where(step == k, bands_ref[0, k], total)
    g0t[...], g0l[...] = halves(total)
    square = (CZ, CZ)
    down = hat((first + iota(square, 0) - 2 * iota(square, 1)).astype(F32), 0.5, 0.25)
    up_out = jnp.where(lane < CZ, first + lane, lane - (128 * gz))
    up = hat((up_out - 2 * row).astype(F32), 1.0, 0.5)
    g1[...] = mm(down.astype(BF16), up.astype(BF16)).astype(BF16)
    step1 = jnp.abs(iota(square, 0) - iota(square, 1))
    total1 = jnp.zeros(square, F32)
    for k in range(1, BANDS + 1):
        total1 = jnp.where(step1 == k, bands_ref[1, k], total1)
    middle = mm_exact_left(down.astype(BF16), total1)
    g2t[...], g2l[...] = halves(mm_exact_right(middle, up.astype(BF16)))
    s1 = (CX * CY, 9 * 24)
    cell, coarse = iota(s1, 0), iota(s1, 1)
    l1[...] = (
        hat((cell // CY - 2 * (coarse // 24)).astype(F32), 1.0, 0.5)
        * hat((cell % CY - 2 * (coarse % 24)).astype(F32), 1.0, 0.5)
    ).astype(BF16)
    s2 = (CX * CY, 9 * CX)
    cell, coarse = iota(s2, 0), iota(s2, 1)
    l2[...] = jnp.where(
        cell // CY == coarse % CX,
        hat((cell % CY - 4 * (coarse // CX)).astype(F32), 1.0, 0.25),
        0.0,
    ).astype(BF16)
    s3 = (8, 128)
    a, from_x = iota(s3, 0), iota(s3, 1)
    offset = (4 * (gx - from_x // 8) + a - from_x % 8 + 128) % 64
    picked = jnp.zeros(s3, F32)
    for o in range(64):
        picked = jnp.where(offset == o, cycle_ref[o], picked)
    s4 = (CX, 8)
    px = hat((iota(s4, 0) - 4 * iota(s4, 1)).astype(F32), 1.0, 0.25)
    cx[...] = lax.dot_general(
        px, picked, (((1,), (0,)), ((), ())), preferred_element_type=F32, precision=HIGH
    )
    s5 = (128, 2 * CZ)
    z, out = iota(s5, 0), iota(s5, 1)
    weight = hat((out % CZ - 4 * (z % 64)).astype(F32), 1.0, 0.25)
    pz[...] = jnp.where((z < 64) == (out < CZ), weight, 0.0).astype(BF16)
    s6 = (CZ, 384)
    layer, out = iota(s6, 0), iota(s6, 1)
    weight = hat((layer - 4 * (out % 64)).astype(F32), 0.25, 0.0625)
    shared = hat((layer - CZ * (1 - gz)).astype(F32), 0.25, 0.0625)
    part = out // 64
    rz[...] = jnp.where(
        (part == 0) | (part == 3), weight, jnp.where(out >= 256, shared, 0.0)
    ).astype(BF16)


def coarse_kernel(arrived, rz, table, message, spread, weights):
    for i in range(ROWS // 128):
        table[pl.ds(i * 128, 128), :] = arrived[:, i * 128 : (i + 1) * 128].T
    layer_ids = fiota((CZ, 128), 0)
    row = iota((80, 128), 0)
    row_y = (row // 8).astype(F32) * 4.0
    row_x = (row % 8).astype(F32) * 4.0
    for n, dy in enumerate((-1, 0, 1)):
        block = block_index(0, dy)

        def chunk(c, carry):
            charge, height, column = atom_rows(table, block, c, 1)
            at = pl.ds(pl.multiple_of((n * CAP + c) * 128, 128), 128)
            spread[:, at] = spread_chunk(charge, height, layer_ids)
            x, y = place_of(column)
            y = y + float(CY * dy)
            weights[:, at] = (
                hat(x - row_x, 0.25, 0.0625) * hat(y - row_y, 0.25, 0.0625)
            ).astype(BF16)
            return carry

        lax.fori_loop(0, CAP, chunk, 0, unroll=4)
    lateral = mm_nt(weights[...], spread[...])
    coarse = mm_exact_right(lateral, rz[...])
    lane = iota((8, 128), 1)
    parts = []
    shared = jnp.zeros((8, 128), F32)
    for t in range(5):
        even = coarse[16 * t : 16 * t + 8, :]
        odd = coarse[16 * t + 8 : 16 * t + 16, :]
        shared = jnp.where(lane == 64 + 2 * t, even[:, 256:384], shared)
        if t < 4:
            shared = jnp.where(lane == 65 + 2 * t, odd[:, 256:384], shared)
            parts.append(even[:, :128] + odd[:, 128:256])
        else:
            parts.append(even[:, :128] + shared)
    for s in range(32):
        for t in range(5):
            message[s, :, t * 128 : (t + 1) * 128] = parts[t]


def local_kernel(bands_ref, table, g0t, g0l, g1, g2t, g2l, l1, base, slab, spread, weights, fine, mid):
    layer_ids = fiota((CZ, 128), 0)
    mid[...] = jnp.zeros(mid.shape, F32)
    for dx in (0, -1, 1):
        for dy in (0, -1, 1):
            block = block_index(dx, dy)
            x0, nx_keep, nx, y0, ny = REACH[dx, dy]
            fine_rows = 0
            if (dx, dy) in FINE:
                fx, fnx, fy, fny = FINE[dx, dy]
                fine_rows = fnx * fny
                cells = iota((fine_rows, 128), 0)
                wanted = ((fx + cells // fny) * CY + fy + cells % fny).astype(F32)
            total_rows = fine_rows + nx * ny
            plane_x = (2.0 * (x0 + iota((nx, 1, 128), 0))).astype(F32)
            row_y = (2.0 * (y0 + iota((ny, 128), 0))).astype(F32)

            def chunk(c, carry):
                charge, height, column = atom_rows(table, block, c, 1)
                at = pl.ds(pl.multiple_of(c * 128, 128), 128)
                spread[:, at] = spread_chunk(charge, height, layer_ids)
                if fine_rows:
                    weights[0:fine_rows, at] = jnp.where(column == wanted, 1.0, 0.0).astype(BF16)
                x, y = place_of(column)
                x = x + float(CX * dx)
                y = y + float(CY * dy)
                wx = hat(x.reshape(1, 1, 128) - plane_x, 0.5, 0.25)
                wy = hat(y - row_y, 0.5, 0.25)
                product = (wx * wy[None]).reshape(nx * ny, 128)
                weights[fine_rows:total_rows, at] = product.astype(BF16)
                return carry

            lax.fori_loop(0, CAP, chunk, 0, unroll=2)
            if fine_rows:
                got = mm_nt(weights[0:fine_rows, :], spread[...]).reshape(fnx, fny, CZ)
                px = {0: 4, -1: 0, 1: 20}[dx]
                py = {0: 8, -1: 0, 1: 40}[dy]
                fine[px : px + fnx, py : py + fny, :] = got
            got = mm_nt(weights[fine_rows:total_rows, :], spread[...]).reshape(nx, ny, CZ)
            keep = (slice(x0 + 4, x0 + 4 + nx_keep), slice(y0 + 8, y0 + 8 + ny))
            mid[keep[0], keep[1], :] += got[:nx_keep]

    own = mid[4:13, 8:32, :]
    lateral = bands_ref[1, 0] * own
    for k in range(1, BANDS + 1):
        lateral += bands_ref[1, k] * (
            (mid[4 + k : 13 + k, 8:32, :] + mid[4 - k : 13 - k, 8:32, :])
            + (mid[4:13, 8 + k : 32 + k, :] + mid[4:13, 8 - k : 32 - k, :])
        )
    coarse = mm_exact_right(lateral.reshape(216, CZ), g1[...])
    coarse += mm_both(own.reshape(216, CZ), g2t[...], g2l[...])
    field = fine[4:20, 8:40, :].reshape(CX * CY, CZ)
    total = mm_exact_left(l1[...], coarse) + mm_both(field, g0t[...], g0l[...])
    slab[...] = total[:, CZ:]
    base[...] = total[:, :CZ]

    def plane(p, carry):
        lateral = jnp.zeros((CY, CZ), F32)
        for k in range(1, BANDS + 1):
            lateral += bands_ref[0, k] * (
                (fine[p + 4 + k, 8:40, :] + fine[p + 4 - k, 8:40, :])
                + (fine[p + 4, 8 + k : 40 + k, :] + fine[p + 4, 8 - k : 40 - k, :])
            )
        base[pl.ds(pl.multiple_of(p * CY, CY), CY), :] += lateral
        return carry

    lax.fori_loop(0, CX, plane, 0)


def last_kernel(where_ref, gathered, base, slab, table, cx, pz, l2, grid, atoms, picked):
    gz = where_ref[1]
    is_upper = gz == 1
    mine = gathered[pl.ds(16 * gz, 16), :, :].reshape(128, MSG)
    other = gathered[pl.ds(16 - 16 * gz, 16), :, MSG - 128 :].reshape(128, 128)

    def conv(v):
        return lax.dot_general(
            cx[...], v, (((1,), (0,)), ((), ())), preferred_element_type=F32, precision=HIGH
        )

    values = conv(mine)
    shared = conv(other)
    lane = iota((CX, 128), 1)
    tail = values[:, MSG - 128 :]
    shared = jnp.where(is_upper, 0.0, tail) + shared
    stacked = jnp.concatenate(
        [values[:, t * 128 : (t + 1) * 128] for t in range(4)] + [jnp.where(lane < 64, tail, 0.0)],
        axis=0,
    )
    layered = mm_exact_right(stacked, pz[...])
    out_layer = iota((1, CZ), 1)
    shared_weight = hat((out_layer - CZ * (1 - gz)).astype(F32), 1.0, 0.25)
    rows = []
    for y in range(9):
        part = layered[(y // 2) * 16 : (y // 2) * 16 + 16, (y % 2) * CZ : (y % 2 + 1) * CZ]
        rows.append(part + shared[:, 64 + y : 65 + y] * shared_weight)
    coarse = jnp.concatenate(rows, axis=0)
    near = slab[...]
    low = jnp.where(is_upper, near, 0.0)
    high = jnp.where(is_upper, 0.0, near)
    potential = base[...] + mm_exact_left(l2[...], coarse) + jnp.concatenate([low, high], axis=1)
    grid[...] = potential.reshape(CX, CY, CZ)
    turned = potential.T.astype(BF16)
    layer_ids = fiota((CZ, 128), 0)
    cells = fiota((CX * CY, 128), 0)

    def chunk(c, carry):
        _, height, column = atom_rows(table, OWN, c, 1)
        one = jnp.where(column == cells, 1.0, 0.0).astype(BF16)
        read = mm(turned, one)
        tent = jnp.maximum(0.0, 1.0 - jnp.abs(layer_ids - height))
        picked[pl.ds(c, 1), :] = jnp.sum(read * tent, axis=0, keepdims=True)
        return carry

    lax.fori_loop(0, CAP, chunk, 0, unroll=2)
    atoms[...] = picked[...].T.reshape(1, 1, SENDERS, CAP)


def vmem():
    return pl.BlockSpec(memory_space=pltpu.VMEM)


def smem():
    return pl.BlockSpec(memory_space=pltpu.SMEM)


def shaped(*pairs):
    return tuple(jax.ShapeDtypeStruct(shape, dtype) for shape, dtype in pairs)


PARAMS = pltpu.CompilerParams(vmem_limit_bytes=VMEM_LIMIT)


def pack(charges, heights, columns, counts):
    live = jnp.arange(CAP, dtype=jnp.int32)[None, :] < counts[:, None]
    own = jnp.concatenate(
        [jnp.where(live, charges, 0.0), heights, jnp.where(live, columns.astype(F32), -1.0)], axis=1
    ).reshape(16, 8, NEAR)
    near = [
        jnp.roll(own, (-dx, -dy), (0, 1)) for dx in (-1, 0, 1) for dy in (-1, 0, 1)
    ]
    near.append(jnp.zeros((16, 8, ROWS - FIELDS), F32))
    return jnp.concatenate(near, axis=2).reshape(SENDERS, ROWS)


def local(charges, heights, columns, counts, bands, cycle_kernel):
    place = jnp.stack([lax.axis_index("gx"), lax.axis_index("gz")]).astype(jnp.int32)
    sent = pack(charges[0, 0], heights[0, 0], columns[0, 0], counts[0, 0])
    arrived = lax.all_to_all(sent, ("gx", "gy"), split_axis=0, concat_axis=0, tiled=True)
    wide = CZ + 128
    g0t, g0l, g1, g2t, g2l, l1, l2, cx, pz, rz = pl.pallas_call(
        tables_kernel,
        in_specs=[smem(), smem(), smem()],
        out_specs=[vmem()] * 10,
        out_shape=shaped(
            ((CZ, wide), BF16),
            ((CZ, wide), BF16),
            ((CZ, wide), BF16),
            ((CZ, wide), BF16),
            ((CZ, wide), BF16),
            ((CX * CY, 216), BF16),
            ((CX * CY, 9 * CX), BF16),
            ((CX, 128), F32),
            ((128, 2 * CZ), BF16),
            ((CZ, 384), BF16),
        ),
        compiler_params=PARAMS,
        name="tables",
    )(place, bands, cycle_kernel)
    table, message = pl.pallas_call(
        coarse_kernel,
        in_specs=[vmem()] * 2,
        out_specs=[vmem()] * 2,
        out_shape=shaped(((ROWS, 128), F32), ((32, 8, MSG), F32)),
        scratch_shapes=[pltpu.VMEM((CZ, 3 * 2048), BF16), pltpu.VMEM((80, 3 * 2048), BF16)],
        compiler_params=PARAMS,
        name="coarse",
    )(arrived, rz)
    gathered = lax.all_to_all(message, ("gz", "gx"), split_axis=0, concat_axis=0, tiled=True)
    base, slab = pl.pallas_call(
        local_kernel,
        in_specs=[smem()] + [vmem()] * 7,
        out_specs=[vmem()] * 2,
        out_shape=shaped(((CX * CY, CZ), F32), ((CX * CY, 128), F32)),
        scratch_shapes=[
            pltpu.VMEM((CZ, 2048), BF16),
            pltpu.VMEM((752, 2048), BF16),
            pltpu.VMEM((24, 48, CZ), F32),
            pltpu.VMEM((17, 40, CZ), F32),
        ],
        compiler_params=PARAMS,
        name="local",
    )(bands, table, g0t, g0l, g1, g2t, g2l, l1)
    slab = lax.ppermute(slab, "gz", [(0, 1), (1, 0)])
    return pl.pallas_call(
        last_kernel,
        in_specs=[smem()] + [vmem()] * 7,
        out_specs=[vmem()] * 2,
        out_shape=shaped(((CX, CY, CZ), F32), ((1, 1, SENDERS, CAP), F32)),
        scratch_shapes=[pltpu.VMEM((CAP, 128), F32)],
        compiler_params=PARAMS,
        name="last",
    )(place, gathered, base, slab, table, cx, pz, l2)


def solution(mesh):
    placed = (
        P("gz", ("gx", "gy"), None, None),
        P("gz", ("gx", "gy"), None, None),
        P("gz", ("gx", "gy"), None, None),
        P("gz", ("gx", "gy"), None),
        P(),
        P(),
    )
    return jax.shard_map(
        local,
        mesh=mesh,
        in_specs=placed,
        out_specs=(P("gx", "gy", "gz"), P("gz", ("gx", "gy"), None, None)),
        check_vma=False,
    )
```

```python
import jax
import jax.numpy as jnp
from jax import lax
from jax.experimental import pallas as pl
from jax.experimental.pallas import tpu as pltpu
from jax.sharding import PartitionSpec as P

CX, CY, CZ, CAP = 16, 32, 256, 16
BANDS = 4
SENDERS = 128
NEAR = 3 * CAP
FIELDS = 9 * NEAR
PLANES = 5
CHUNKS = 5
MSG = 32
F32, BF16 = jnp.float32, jnp.bfloat16
HIGH = lax.Precision.HIGHEST
VMEM_LIMIT = 48 * 1024 * 1024

OWN = 4
REACH = {
    (0, 0): (0, 9, 10, 0, 24),
    (-1, 0): (-4, 5, 6, 0, 24),
    (1, 0): (8, 5, 6, 0, 24),
    (0, -1): (0, 9, 9, -8, 16),
    (0, 1): (0, 9, 10, 16, 8),
    (-1, -1): (-4, 5, 5, -8, 16),
    (-1, 1): (-4, 5, 6, 16, 8),
    (1, -1): (8, 5, 5, -8, 16),
    (1, 1): (8, 5, 6, 16, 8),
}
FINE = {
    (0, 0): (0, 16, 0, 32),
    (-1, 0): (12, 4, 0, 32),
    (1, 0): (0, 4, 0, 32),
    (0, -1): (0, 16, 24, 8),
    (0, 1): (0, 16, 0, 8),
}


def iota(shape, dim):
    return lax.broadcasted_iota(jnp.int32, shape, dim)


def fiota(shape, dim):
    return iota(shape, dim).astype(F32)


def hat(distance, peak, slope):
    return jnp.maximum(0.0, peak - slope * jnp.abs(distance))


def mm(a, b):
    return lax.dot_general(a, b, (((1,), (0,)), ((), ())), preferred_element_type=F32)


def mm_nt(a, b):
    return lax.dot_general(a, b, (((1,), (1,)), ((), ())), preferred_element_type=F32)


def halves(a):
    top = a.astype(BF16)
    return top, (a - top.astype(F32)).astype(BF16)


def mm_exact_right(a, b):
    return mm(jnp.concatenate(halves(a), axis=1), jnp.concatenate([b, b], axis=0))


def mm_exact_left(a, b):
    return mm(jnp.concatenate([a, a], axis=1), jnp.concatenate(halves(b), axis=0))


def block_index(dx, dy):
    return (dx + 1) * 3 + dy + 1


def atom_rows(table, block, first, count):
    base = block * NEAR + first
    return (
        table[pl.ds(base, count), :],
        table[pl.ds(base + CAP, count), :],
        table[pl.ds(base + 2 * CAP, count), :],
    )


def tent_rows(charge, height):
    floor = jnp.floor(height)
    above = floor + 1.0
    low = charge * jnp.maximum(0.0, 1.0 - jnp.abs(floor - height))
    high = charge * jnp.maximum(0.0, 1.0 - jnp.abs(above - height))
    return floor, above, low, high


def tall(rows, c, count):
    one = jnp.broadcast_to(rows[c : c + 1], (16, 128)).astype(BF16)
    return jnp.concatenate([one] * (count // 16), axis=0)


def spread_chunk(floor, above, low, high, c, layer_ids):
    rest = jnp.where(layer_ids == tall(above, c, CZ), tall(high, c, CZ), jnp.zeros((), BF16))
    return jnp.where(layer_ids == tall(floor, c, CZ), tall(low, c, CZ), rest)


def place_of(column):
    x = jnp.floor(column * (1.0 / CY))
    return x, column - CY * x


def tables_kernel(where_ref, bands_ref, cycle_ref, g0t, g0l, g1, g2t, g2l, l1, l2, cx, pz):
    gx, gz = where_ref[0], where_ref[1]
    wide = CZ + 128
    shape = (CZ, wide)
    row = iota(shape, 0)
    lane = iota(shape, 1)
    first = CZ * gz
    out_layer = jnp.where(lane < CZ, first + lane, lane - (128 * gz))
    step = jnp.abs(first + row - out_layer)
    zero = jnp.zeros(shape, F32)
    total = jnp.where(step == 0, bands_ref[0, 0], zero)
    for k in range(1, BANDS + 1):
        total = jnp.where(step == k, bands_ref[0, k], total)
    g0t[...], g0l[...] = halves(total)
    square = (CZ, CZ)
    down = hat((first + iota(square, 0) - 2 * iota(square, 1)).astype(F32), 0.5, 0.25)
    up_out = jnp.where(lane < CZ, first + lane, lane - (128 * gz))
    up = hat((up_out - 2 * row).astype(F32), 1.0, 0.5)
    g1[...] = mm(down.astype(BF16), up.astype(BF16)).astype(BF16)
    step1 = jnp.abs(iota(square, 0) - iota(square, 1))
    total1 = jnp.zeros(square, F32)
    for k in range(1, BANDS + 1):
        total1 = jnp.where(step1 == k, bands_ref[1, k], total1)
    middle = mm_exact_left(down.astype(BF16), total1)
    g2t[...], g2l[...] = halves(mm_exact_right(middle, up.astype(BF16)))
    s1 = (CX * CY, CZ)
    cell, coarse = iota(s1, 0), iota(s1, 1)
    product = hat((cell // CY - 2 * (coarse // 24)).astype(F32), 1.0, 0.5) * hat(
        (cell % CY - 2 * (coarse % 24)).astype(F32), 1.0, 0.5
    )
    l1[...] = jnp.where(coarse < 9 * 24, product, 0.0).astype(BF16)
    s2 = (CX * CY, 2 * 9 * CX)
    cell, coarse = iota(s2, 0), iota(s2, 1) % (9 * CX)
    l2[...] = jnp.where(
        cell // CY == coarse % CX,
        hat((cell % CY - 4 * (coarse // CX)).astype(F32), 1.0, 0.25),
        0.0,
    ).astype(BF16)
    s3 = (8, 16 * MSG)
    a, source = iota(s3, 0), iota(s3, 1)
    offset = (4 * (gx - source // MSG) + a - source % MSG % PLANES + 128) % 64
    picked = jnp.zeros(s3, F32)
    for o in range(64):
        picked = jnp.where(offset == o, cycle_ref[o], picked)
    s4 = (CX, 8)
    px = hat((iota(s4, 0) - 4 * iota(s4, 1)).astype(F32), 1.0, 0.25)
    turned = lax.dot_general(
        px, picked, (((1,), (0,)), ((), ())), preferred_element_type=F32, precision=HIGH
    )
    chunk = iota((CX, 16 * MSG), 1) % MSG // PLANES
    count = 16 * MSG
    for t in range(CHUNKS):
        top, low = halves(jnp.where(chunk == t, turned, 0.0))
        rows = slice(t * CX, (t + 1) * CX)
        cx[rows, 0:count] = top
        cx[rows, count : 2 * count] = low
        cx[rows, 2 * count :] = top
    s5 = (128, 2 * CZ)
    z, out = iota(s5, 0), iota(s5, 1)
    weight = hat((out % CZ - 4 * (z % 64)).astype(F32), 1.0, 0.25)
    pz[...] = jnp.where((z < 64) == (out < CZ), weight, 0.0).astype(BF16)


def pack_kernel(charges_in, heights_in, columns_in, counts_in, message, charges, heights, columns, counts, done):
    pairs = ((counts_in, counts), (charges_in, charges), (columns_in, columns), (heights_in, heights))
    copies = [pltpu.make_async_copy(a, b, done.at[i]) for i, (a, b) in enumerate(pairs)]
    for copy in copies:
        copy.start()
    for copy in copies:
        copy.wait()
    live = iota((CAP, SENDERS), 0) < counts[...]
    own = jnp.concatenate(
        [
            jnp.where(live, charges[...], 0.0),
            heights[...],
            jnp.where(live, columns[...].astype(F32), -1.0),
        ],
        axis=0,
    )
    ring = iota((NEAR, SENDERS), 1) % 8
    below = jnp.where(ring == 0, pltpu.roll(own, SENDERS - 7, 1), pltpu.roll(own, 1, 1))
    above = jnp.where(ring == 7, pltpu.roll(own, 7, 1), pltpu.roll(own, SENDERS - 1, 1))
    near = []
    for turn in (8, 0, SENDERS - 8):
        for part in (below, own, above):
            near.append(pltpu.roll(part, turn, 1) if turn else part)
    table = jnp.concatenate(near, axis=0)
    for i in range(0, FIELDS, 128):
        at = slice(i, min(i + 128, FIELDS))
        message[:, 0, at] = table[at, :].T


def coarse_kernel(where_ref, arrived, table, message, spread, weights):
    gz = where_ref[1]
    for i in range(0, FIELDS, 128):
        at = slice(i, min(i + 128, FIELDS))
        table[at, :] = arrived[:, 0, at].T
    layer_ids = fiota((CZ, 128), 0).astype(BF16)
    cell_x = 4.0 * fiota((8, 128), 0)
    cell_y = 4.0 * fiota((10, 128), 0)
    lateral = jnp.zeros((80, CZ), F32)
    for n, dy in enumerate((-1, 0, 1)):
        charge, height, column = atom_rows(table, block_index(0, dy), 0, CAP)
        floor, above, low, high = tent_rows(charge, height)
        x, y = place_of(column)
        y = y + float(CY * dy)
        for c in range(CAP):
            at = slice((n * CAP + c) * 128, (n * CAP + c + 1) * 128)
            spread[:, at] = spread_chunk(floor, above, low, high, c, layer_ids)
            wx = hat(x[c : c + 1] - cell_x, 0.25, 0.0625)
            wy = hat(y[c : c + 1] - cell_y, 0.25, 0.0625)
            weights[:, at] = (wy[:, None, :] * wx[None]).reshape(80, 128).astype(BF16)
            if c % 8 == 7:
                half = slice((n * CAP + c - 7) * 128, (n * CAP + c + 1) * 128)
                lateral += mm_nt(weights[:, half], spread[:, half])
    layer, out = iota((CZ, 128), 0), iota((CZ, 128), 1)
    down = hat((layer - jnp.where(out < 64, 4 * out, CZ * (1 - gz))).astype(F32), 0.25, 0.0625)
    coarse = mm_exact_right(lateral, down.astype(BF16))
    lane = iota((8, 128), 1)
    tiles = [coarse[8 * y : 8 * y + 8, :] for y in range(9)]
    parts = [
        jnp.where(lane < 64, tiles[2 * t], pltpu.roll(tiles[2 * t + 1], 64, 1)) for t in range(4)
    ]
    last = tiles[8]
    for y in range(9):
        moved = pltpu.roll(tiles[y], y, 1) if y else tiles[y]
        last = jnp.where(lane == 64 + y, moved, last)
    parts.append(jnp.where(lane < 64 + 9, last, 0.0))
    packed = jnp.concatenate(
        [part[:PLANES] for part in parts] + [jnp.zeros((MSG - PLANES * CHUNKS, 128), F32)], axis=0
    )
    for s in range(32):
        message[s] = packed


def fine_key(dx, dy, column, x, y):
    if dx:
        return [column - float(CX * CY - 128) if dx < 0 else column]
    if dy:
        local_y = y - float(CY - 8) if dy < 0 else y
        inside = (local_y >= 0.0) & (local_y < 8.0)
        return [jnp.where(inside, 8.0 * x + local_y, -1.0)]
    return [column, column - 256.0]


def local_kernel(bands_ref, table, g0t, g0l, g1, g2t, g2l, l1, slab, fine, inner, spread, weights, mid):
    layer_ids = fiota((CZ, 128), 0).astype(BF16)
    mid[4:13, 32:40, :] = jnp.zeros((9, 8, CZ), F32)
    order = [(0, 0), (-1, 0), (1, 0), (0, -1), (0, 1), (-1, -1), (-1, 1), (1, -1), (1, 1)]
    for n, (dx, dy) in enumerate(order):
        turn = n % 2
        charge, height, column = atom_rows(table, block_index(dx, dy), 0, CAP)
        floor, above, low, high = tent_rows(charge, height)
        x, y = place_of(column)
        keys = fine_key(dx, dy, column, x, y) if (dx, dy) in FINE else []
        x = x + float(CX * dx)
        y = y + float(CY * dy)
        x0, nx_keep, nx, y0, ny = REACH[dx, dy]
        page = CZ if (dx, dy) == (0, 0) else 128
        fine_rows = page * len(keys)
        total_rows = fine_rows + nx * ny
        plane_x = 2.0 * (float(x0) + fiota((nx, 128), 0))
        row_y = 2.0 * (float(y0) + fiota((ny, 128), 0))
        for c in range(CAP):
            at = slice(c * 128, (c + 1) * 128)
            spread[turn, :, at] = spread_chunk(floor, above, low, high, c, layer_ids)
            for i, key in enumerate(keys):
                match = layer_ids[:page] == tall(key, c, page)
                weights[turn, i * page : (i + 1) * page, at] = jnp.where(
                    match, jnp.ones((), BF16), jnp.zeros((), BF16)
                )
            wx = hat(x[c : c + 1] - plane_x, 0.5, 0.25)
            wy = hat(y[c : c + 1] - row_y, 0.5, 0.25)
            product = (wx[:, None, :] * wy[None]).reshape(nx * ny, 128)
            weights[turn, fine_rows:total_rows, at] = product.astype(BF16)
        got = mm_nt(weights[turn, 0:total_rows, :], spread[turn])
        if keys:
            _, fnx, _, fny = FINE[dx, dy]
            px = {0: 4, -1: 0, 1: 20}[dx]
            py = {0: 8, -1: 0, 1: 40}[dy]
            fine[px : px + fnx, py : py + fny, :] = got[:fine_rows].reshape(fnx, fny, CZ)
        got = got[fine_rows:].reshape(nx, ny, CZ)[:nx_keep]
        new_x = {0: (0, 9), -1: (0, 4), 1: (1, 5)}[dx] if dy == 0 else (0, 0)
        if (dx, dy) == (0, -1):
            mid[4:13, 0:8, :] = got[:, :8]
            mid[4:13, 8:16, :] += got[:, 8:]
            continue
        for i in range(nx_keep):
            at = (x0 + 4 + i, slice(y0 + 8, y0 + 8 + ny))
            if new_x[0] <= i < new_x[1]:
                mid[at[0], at[1], :] = got[i]
            else:
                mid[at[0], at[1], :] += got[i]

    own = mid[4:13, 8:32, :]
    lateral = bands_ref[1, 0] * own
    for k in range(1, BANDS + 1):
        lateral += bands_ref[1, k] * (
            (mid[4 + k : 13 + k, 8:32, :] + mid[4 - k : 13 - k, 8:32, :])
            + (mid[4:13, 8 + k : 32 + k, :] + mid[4:13, 8 - k : 32 - k, :])
        )
    side_top, side_low = halves(lateral.reshape(216, CZ))
    own_top, own_low = halves(own.reshape(216, CZ))
    coarse = mm(
        jnp.concatenate([side_top, side_low, own_top, own_low, own_top], axis=1),
        jnp.concatenate([g1[...], g1[...], g2t[...], g2t[...], g2l[...]], axis=0),
    )
    coarse = jnp.concatenate([coarse, jnp.zeros((CZ - 216, CZ + 128), F32)], axis=0)
    coarse_top, coarse_low = halves(coarse)
    inner[...] = jnp.concatenate([coarse_top[:, :CZ], coarse_low[:, :CZ]], axis=0)
    field_top, field_low = halves(fine[4:20, 8:40, :].reshape(CX * CY, CZ))
    slab[...] = mm(
        jnp.concatenate([l1[...], l1[...], field_top, field_low, field_top], axis=1),
        jnp.concatenate(
            [coarse_top[:, CZ:], coarse_low[:, CZ:], g0t[:, CZ:], g0t[:, CZ:], g0l[:, CZ:]], axis=0
        ),
    )


def base_kernel(bands_ref, fine, inner, g0t, g0l, l1, base):
    field_top, field_low = halves(fine[4:20, 8:40, :].reshape(CX * CY, CZ))
    base[...] = mm(
        jnp.concatenate([l1[...], l1[...], field_top, field_low, field_top], axis=1),
        jnp.concatenate([inner[...], g0t[:, :CZ], g0t[:, :CZ], g0l[:, :CZ]], axis=0),
    )
    for p in range(CX):
        lateral = jnp.zeros((CY, CZ), F32)
        for k in range(1, BANDS + 1):
            lateral += bands_ref[0, k] * (
                (fine[p + 4 + k, 8:40, :] + fine[p + 4 - k, 8:40, :])
                + (fine[p + 4, 8 + k : 40 + k, :] + fine[p + 4, 8 - k : 40 - k, :])
            )
        base[p * CY : (p + 1) * CY, :] += lateral


def last_kernel(where_ref, gathered, base, slab, table, cx, pz, l2, grid, atoms):
    gz = where_ref[1]
    is_upper = gz == 1
    mine = gathered[pl.ds(16 * gz, 16), :, :].reshape(16 * MSG, 128)
    other = gathered[pl.ds(16 - 16 * gz, 16), :, :].reshape(16 * MSG, 128)

    def conv(table, v):
        top, low = halves(v)
        return mm(table, jnp.concatenate([top, top, low], axis=0))

    values = conv(cx[...], mine)
    shared = conv(cx[4 * CX :, :], other)
    lane = iota((CX, 128), 1)
    tail = values[4 * CX :]
    shared = jnp.where(is_upper, 0.0, tail) + shared
    stacked = jnp.concatenate([values[: 4 * CX], jnp.where(lane < 64, tail, 0.0)], axis=0)
    layered = mm_exact_right(stacked, pz[...])
    out_layer = iota((1, CZ), 1)
    shared_weight = hat((out_layer - CZ * (1 - gz)).astype(F32), 1.0, 0.25)
    rows = []
    for y in range(9):
        part = layered[(y // 2) * 16 : (y // 2) * 16 + 16, (y % 2) * CZ : (y % 2 + 1) * CZ]
        rows.append(part + shared[:, 64 + y : 65 + y] * shared_weight)
    coarse = jnp.concatenate(rows, axis=0)
    near = slab[...]
    low = jnp.where(is_upper, near, 0.0)
    high = jnp.where(is_upper, 0.0, near)
    potential = base[...] + mm(l2[...], jnp.concatenate(halves(coarse), axis=0)) + jnp.concatenate([low, high], axis=1)
    grid[...] = potential.reshape(CX, CY, CZ)
    turned = potential.T.astype(BF16)
    _, height, column = atom_rows(table, OWN, 0, CAP)
    layer_ids = fiota((CZ, 128), 0)
    row_ids = layer_ids.astype(BF16)
    keys = fine_key(0, 0, column, None, None)
    for c in range(0, CAP, 2):
        one = [
            jnp.concatenate(
                [
                    jnp.where(row_ids == tall(key, d, CZ), jnp.ones((), BF16), jnp.zeros((), BF16))
                    for key in keys
                ],
                axis=0,
            )
            for d in (c, c + 1)
        ]
        read = mm(turned, jnp.concatenate(one, axis=1))
        for i, d in enumerate((c, c + 1)):
            tent = jnp.maximum(0.0, 1.0 - jnp.abs(layer_ids - height[d : d + 1]))
            atoms[d : d + 1, :] = jnp.sum(
                read[:, i * 128 : (i + 1) * 128] * tent, axis=0, keepdims=True
            )


def vmem():
    return pl.BlockSpec(memory_space=pltpu.VMEM)


def smem():
    return pl.BlockSpec(memory_space=pltpu.SMEM)


def shaped(*pairs):
    return tuple(jax.ShapeDtypeStruct(shape, dtype) for shape, dtype in pairs)


PARAMS = pltpu.CompilerParams(vmem_limit_bytes=VMEM_LIMIT)


def local(charges, heights, columns, counts, bands, cycle_kernel):
    place = jnp.stack([lax.axis_index("gx"), lax.axis_index("gz")]).astype(jnp.int32)
    sent = pl.pallas_call(
        pack_kernel,
        in_specs=[pl.BlockSpec(memory_space=pltpu.HBM)] * 4,
        out_specs=vmem(),
        out_shape=jax.ShapeDtypeStruct((SENDERS, 1, FIELDS), F32),
        scratch_shapes=[
            pltpu.VMEM((CAP, SENDERS), F32),
            pltpu.VMEM((CAP, SENDERS), F32),
            pltpu.VMEM((CAP, SENDERS), jnp.int32),
            pltpu.VMEM((1, SENDERS), jnp.int32),
            pltpu.SemaphoreType.DMA((4,)),
        ],
        name="pack",
    )(charges[0, 0].T, heights[0, 0].T, columns[0, 0].T, counts[0])
    arrived = lax.all_to_all(sent, ("gx", "gy"), split_axis=0, concat_axis=0, tiled=True)
    wide = CZ + 128
    g0t, g0l, g1, g2t, g2l, l1, l2, cx, pz = pl.pallas_call(
        tables_kernel,
        in_specs=[smem(), smem(), smem()],
        out_specs=[vmem()] * 9,
        out_shape=shaped(
            ((CZ, wide), BF16),
            ((CZ, wide), BF16),
            ((CZ, wide), BF16),
            ((CZ, wide), BF16),
            ((CZ, wide), BF16),
            ((CX * CY, CZ), BF16),
            ((CX * CY, 2 * 9 * CX), BF16),
            ((CHUNKS * CX, 3 * 16 * MSG), BF16),
            ((128, 2 * CZ), BF16),
        ),
        compiler_params=PARAMS,
        name="tables",
    )(place, bands, cycle_kernel)
    arrived, g0t, g0l, g1, g2t, g2l, l1, l2, cx, pz = lax.optimization_barrier(
        (arrived, g0t, g0l, g1, g2t, g2l, l1, l2, cx, pz)
    )
    table, message = pl.pallas_call(
        coarse_kernel,
        in_specs=[smem(), vmem()],
        out_specs=[vmem()] * 2,
        out_shape=shaped(((FIELDS, 128), F32), ((32, MSG, 128), F32)),
        scratch_shapes=[pltpu.VMEM((CZ, 3 * 2048), BF16), pltpu.VMEM((80, 3 * 2048), BF16)],
        compiler_params=PARAMS,
        name="coarse",
    )(place, arrived)
    gathered = lax.all_to_all(message, ("gz", "gx"), split_axis=0, concat_axis=0, tiled=True)
    slab, fine, inner = pl.pallas_call(
        local_kernel,
        in_specs=[smem()] + [vmem()] * 7,
        out_specs=[vmem()] * 3,
        out_shape=shaped(
            ((CX * CY, 128), F32),
            ((CX + 2 * BANDS, CY + 16, CZ), F32),
            ((2 * CZ, CZ), BF16),
        ),
        scratch_shapes=[
            pltpu.VMEM((2, CZ, 2048), BF16),
            pltpu.VMEM((2, 752, 2048), BF16),
            pltpu.VMEM((17, 40, CZ), F32),
        ],
        compiler_params=PARAMS,
        name="local",
    )(bands, table, g0t, g0l, g1, g2t, g2l, l1)
    slab = lax.ppermute(slab, "gz", [(0, 1), (1, 0)])
    base = pl.pallas_call(
        base_kernel,
        in_specs=[smem()] + [vmem()] * 5,
        out_specs=vmem(),
        out_shape=jax.ShapeDtypeStruct((CX * CY, CZ), F32),
        compiler_params=PARAMS,
        cost_estimate=pl.CostEstimate(flops=10**9, bytes_accessed=4 * 10**6, transcendentals=0),
        name="base",
    )(bands, fine, inner, g0t, g0l, l1)
    grid, atoms = pl.pallas_call(
        last_kernel,
        in_specs=[smem()] + [vmem()] * 7,
        out_specs=[vmem()] * 2,
        out_shape=shaped(((CX, CY, CZ), F32), ((CAP, SENDERS), F32)),
        compiler_params=PARAMS,
        name="last",
    )(place, gathered, base, slab, table, cx, pz, l2)
    return grid, atoms.T[None, None]


def solution(mesh):
    placed = (
        P("gz", ("gx", "gy"), None, None),
        P("gz", ("gx", "gy"), None, None),
        P("gz", ("gx", "gy"), None, None),
        P("gz", ("gx", "gy"), None),
        P(),
        P(),
    )
    return jax.shard_map(
        local,
        mesh=mesh,
        in_specs=placed,
        out_specs=(P("gx", "gy", "gz"), P("gz", ("gx", "gy"), None, None)),
        check_vma=False,
    )
```

```python
import jax
import jax.numpy as jnp
from jax import lax
from jax.experimental import pallas as pl
from jax.experimental.pallas import tpu as pltpu
from jax.sharding import PartitionSpec as P

CX, CY, CZ, CAP = 16, 32, 256, 16
BANDS = 4
SENDERS = 128
NEAR = 3 * CAP
FIELDS = 9 * NEAR
PLANES = 5
MSG = 24
FOLDED = 4 * PLANES
TABLE_ROWS = (4 + 2 + PLANES) * CX
F32, BF16 = jnp.float32, jnp.bfloat16
HIGH = lax.Precision.HIGHEST
VMEM_LIMIT = 48 * 1024 * 1024

OWN = 4
REACH = {
    (0, 0): (0, 9, 10, 0, 24),
    (-1, 0): (-4, 5, 6, 0, 24),
    (1, 0): (8, 5, 6, 0, 24),
    (0, -1): (0, 9, 9, -8, 16),
    (0, 1): (0, 9, 10, 16, 8),
    (-1, -1): (-4, 5, 5, -8, 16),
    (-1, 1): (-4, 5, 6, 16, 8),
    (1, -1): (8, 5, 5, -8, 16),
    (1, 1): (8, 5, 6, 16, 8),
}
FINE = {
    (0, 0): (0, 16, 0, 32),
    (-1, 0): (12, 4, 0, 32),
    (1, 0): (0, 4, 0, 32),
    (0, -1): (0, 16, 24, 8),
    (0, 1): (0, 16, 0, 8),
}


def iota(shape, dim):
    return lax.broadcasted_iota(jnp.int32, shape, dim)


def fiota(shape, dim):
    return iota(shape, dim).astype(F32)


def hat(distance, peak, slope):
    return jnp.maximum(0.0, peak - slope * jnp.abs(distance))


def mm(a, b):
    return lax.dot_general(a, b, (((1,), (0,)), ((), ())), preferred_element_type=F32)


def mm_nt(a, b):
    return lax.dot_general(a, b, (((1,), (1,)), ((), ())), preferred_element_type=F32)


def halves(a):
    top = a.astype(BF16)
    return top, (a - top.astype(F32)).astype(BF16)


def mm_exact_right(a, b):
    return mm(jnp.concatenate(halves(a), axis=1), jnp.concatenate([b, b], axis=0))


def mm_exact_left(a, b):
    return mm(jnp.concatenate([a, a], axis=1), jnp.concatenate(halves(b), axis=0))


def block_index(dx, dy):
    return (dx + 1) * 3 + dy + 1


def atom_rows(table, block, first, count):
    base = block * NEAR + first
    return (
        table[pl.ds(base, count), :],
        table[pl.ds(base + CAP, count), :],
        table[pl.ds(base + 2 * CAP, count), :],
    )


def tent_rows(charge, height):
    floor = jnp.floor(height)
    above = floor + 1.0
    low = charge * jnp.maximum(0.0, 1.0 - jnp.abs(floor - height))
    high = charge * jnp.maximum(0.0, 1.0 - jnp.abs(above - height))
    return floor, above, low, high


def tall(rows, c, count):
    one = jnp.broadcast_to(rows[c : c + 1], (16, 128)).astype(BF16)
    return jnp.concatenate([one] * (count // 16), axis=0)


def spread_chunk(floor, above, low, high, c, layer_ids):
    rest = jnp.where(layer_ids == tall(above, c, CZ), tall(high, c, CZ), jnp.zeros((), BF16))
    return jnp.where(layer_ids == tall(floor, c, CZ), tall(low, c, CZ), rest)


def place_of(column):
    x = jnp.floor(column * (1.0 / CY))
    return x, column - CY * x


def tables_kernel(where_ref, bands_ref, cycle_ref, g0t, g0l, g1, g2t, g2l, l1, l2, cx, pz):
    gx, gz = where_ref[0], where_ref[1]
    wide = CZ + 128
    shape = (CZ, wide)
    row = iota(shape, 0)
    lane = iota(shape, 1)
    first = CZ * gz
    out_layer = jnp.where(lane < CZ, first + lane, lane - (128 * gz))
    step = jnp.abs(first + row - out_layer)
    zero = jnp.zeros(shape, F32)
    total = jnp.where(step == 0, bands_ref[0, 0], zero)
    for k in range(1, BANDS + 1):
        total = jnp.where(step == k, bands_ref[0, k], total)
    g0t[...], g0l[...] = halves(total)
    square = (CZ, CZ)
    down = hat((first + iota(square, 0) - 2 * iota(square, 1)).astype(F32), 0.5, 0.25)
    up_out = jnp.where(lane < CZ, first + lane, lane - (128 * gz))
    up = hat((up_out - 2 * row).astype(F32), 1.0, 0.5)
    g1[...] = mm(down.astype(BF16), up.astype(BF16)).astype(BF16)
    step1 = jnp.abs(iota(square, 0) - iota(square, 1))
    total1 = jnp.zeros(square, F32)
    for k in range(1, BANDS + 1):
        total1 = jnp.where(step1 == k, bands_ref[1, k], total1)
    middle = mm_exact_left(down.astype(BF16), total1)
    g2t[...], g2l[...] = halves(mm_exact_right(middle, up.astype(BF16)))
    s1 = (CX * CY, CZ)
    cell, coarse = iota(s1, 0), iota(s1, 1)
    product = hat((cell // CY - 2 * (coarse // 24)).astype(F32), 1.0, 0.5) * hat(
        (cell % CY - 2 * (coarse % 24)).astype(F32), 1.0, 0.5
    )
    l1[...] = jnp.where(coarse < 9 * 24, product, 0.0).astype(BF16)
    s2 = (CX * CY, 2 * 9 * CX)
    cell, coarse = iota(s2, 0), iota(s2, 1) % (9 * CX)
    l2[...] = jnp.where(
        cell // CY == coarse % CX,
        hat((cell % CY - 4 * (coarse // CX)).astype(F32), 1.0, 0.25),
        0.0,
    ).astype(BF16)
    s3 = (8, 16 * MSG)
    a, source = iota(s3, 0), iota(s3, 1)
    s4 = (CX, 8)
    px = hat((iota(s4, 0) - 4 * iota(s4, 1)).astype(F32), 1.0, 0.25)
    row = source % MSG
    late = 2 * (row - FOLDED)

    def circulant(plane):
        offset = (4 * (gx - source // MSG) + a - plane + 128) % 64
        picked = jnp.zeros(s3, F32)
        for o in range(64):
            picked = jnp.where(offset == o, cycle_ref[o], picked)
        return lax.dot_general(
            px, picked, (((1,), (0,)), ((), ())), preferred_element_type=F32, precision=HIGH
        )

    even = circulant(jnp.where(row < FOLDED, row % PLANES, late))
    odd = circulant(late + 1)
    at = iota((CX, 16 * MSG), 1) % MSG
    pieces = [jnp.where(at // PLANES == t, even, 0.0) for t in range(4)]
    pieces.append(jnp.where((at >= FOLDED) & (at < FOLDED + 3), even, 0.0))
    pieces.append(jnp.where((at >= FOLDED) & (at < FOLDED + 2), odd, 0.0))
    for b in range(PLANES):
        pieces.append(jnp.where(at == FOLDED + 2, circulant(b), 0.0))
    count = 16 * MSG
    for i, piece in enumerate(pieces):
        top, low = halves(piece)
        rows = slice(i * CX, (i + 1) * CX)
        cx[rows, 0:count] = top
        cx[rows, count : 2 * count] = low
        cx[rows, 2 * count :] = top
    s5 = (128, 2 * CZ)
    z, out = iota(s5, 0), iota(s5, 1)
    weight = hat((out % CZ - 4 * (z % 64)).astype(F32), 1.0, 0.25)
    pz[...] = jnp.where((z < 64) == (out < CZ), weight, 0.0).astype(BF16)


def pack_kernel(charges_in, heights_in, columns_in, counts_in, message, charges, heights, columns, counts, done):
    pairs = ((counts_in, counts), (charges_in, charges), (columns_in, columns), (heights_in, heights))
    copies = [pltpu.make_async_copy(a, b, done.at[i]) for i, (a, b) in enumerate(pairs)]
    for copy in copies:
        copy.start()
    for copy in copies:
        copy.wait()
    live = iota((CAP, SENDERS), 0) < counts[...]
    own = jnp.concatenate(
        [
            jnp.where(live, charges[...], 0.0),
            heights[...],
            jnp.where(live, columns[...].astype(F32), -1.0),
        ],
        axis=0,
    )
    ring = iota((NEAR, SENDERS), 1) % 8
    below = jnp.where(ring == 0, pltpu.roll(own, SENDERS - 7, 1), pltpu.roll(own, 1, 1))
    above = jnp.where(ring == 7, pltpu.roll(own, 7, 1), pltpu.roll(own, SENDERS - 1, 1))
    near = []
    for turn in (8, 0, SENDERS - 8):
        for part in (below, own, above):
            near.append(pltpu.roll(part, turn, 1) if turn else part)
    table = jnp.concatenate(near, axis=0)
    for i in range(0, FIELDS, 128):
        at = slice(i, min(i + 128, FIELDS))
        message[:, 0, at] = table[at, :].T


def coarse_kernel(where_ref, arrived, table, message):
    gz = where_ref[1]
    for i in range(0, FIELDS, 128):
        at = slice(i, min(i + 128, FIELDS))
        table[at, :] = arrived[:, 0, at].T
    layer_ids = fiota((CZ, 128), 0).astype(BF16)
    cell_x = 4.0 * fiota((8, 128), 0)
    cell_y = 4.0 * fiota((10, 128), 0)
    spread, weights = [], []
    for dy in (-1, 0, 1):
        charge, height, column = atom_rows(table, block_index(0, dy), 0, CAP)
        floor, above, low, high = tent_rows(charge, height)
        x, y = place_of(column)
        y = y + float(CY * dy)
        for c in range(CAP):
            spread.append(spread_chunk(floor, above, low, high, c, layer_ids))
            wx = hat(x[c : c + 1] - cell_x, 0.25, 0.0625)
            wy = hat(y[c : c + 1] - cell_y, 0.25, 0.0625)
            weights.append((wy[:, None, :] * wx[None]).reshape(80, 128).astype(BF16))
    lateral = mm_nt(jnp.concatenate(weights, axis=1), jnp.concatenate(spread, axis=1))
    layer, out = iota((CZ, 128), 0), iota((CZ, 128), 1)
    down = hat((layer - jnp.where(out < 64, 4 * out, CZ * (1 - gz))).astype(F32), 0.25, 0.0625)
    coarse = mm_exact_right(lateral, down.astype(BF16))
    lane = iota((8, 128), 1)
    tiles = [coarse[8 * y : 8 * y + 8, :] for y in range(9)]
    parts = [
        jnp.where(lane < 64, tiles[2 * t], pltpu.roll(tiles[2 * t + 1], 64, 1)) for t in range(4)
    ]
    shared = jnp.zeros((8, 128), F32)
    for y in range(9):
        shared = jnp.where(lane == 64 + y, pltpu.roll(tiles[y], y, 1) if y else tiles[y], shared)
    turned = pltpu.roll(tiles[8], 64, 1)
    row = lane[:1]
    beside = jnp.zeros((1, 128), F32)
    for b in range(PLANES):
        moved = pltpu.roll(shared, 9 * b, 1) if b else shared
        beside = jnp.where((row >= 64 + 9 * b) & (row < 73 + 9 * b), moved[b : b + 1], beside)
    folded = [
        jnp.where(row < 64, tiles[8][0:1], turned[1:2]),
        jnp.where(row < 64, tiles[8][2:3], turned[3:4]),
        jnp.where(row < 64, tiles[8][4:5], beside),
        jnp.zeros((1, 128), F32),
    ]
    packed = jnp.concatenate([part[:PLANES] for part in parts] + folded, axis=0)
    for s in range(32):
        message[s] = packed


def fine_key(dx, dy, column, x, y):
    if dx:
        return [column - float(CX * CY - 128) if dx < 0 else column]
    if dy:
        local_y = y - float(CY - 8) if dy < 0 else y
        inside = (local_y >= 0.0) & (local_y < 8.0)
        return [jnp.where(inside, 8.0 * x + local_y, -1.0)]
    return [column, column - 256.0]


def local_kernel(bands_ref, table, g0t, g0l, g1, g2t, g2l, l1, slab, fine, inner, mid):
    layer_ids = fiota((CZ, 128), 0).astype(BF16)
    mid[4:13, 32:40, :] = jnp.zeros((9, 8, CZ), F32)
    order = [(0, 0), (-1, 0), (1, 0), (0, -1), (0, 1), (-1, -1), (-1, 1), (1, -1), (1, 1)]
    for n, (dx, dy) in enumerate(order):
        spread, weights = [], []
        charge, height, column = atom_rows(table, block_index(dx, dy), 0, CAP)
        floor, above, low, high = tent_rows(charge, height)
        x, y = place_of(column)
        keys = fine_key(dx, dy, column, x, y) if (dx, dy) in FINE else []
        x = x + float(CX * dx)
        y = y + float(CY * dy)
        x0, nx_keep, nx, y0, ny = REACH[dx, dy]
        page = CZ if (dx, dy) == (0, 0) else 128
        fine_rows = page * len(keys)
        plane_x = 2.0 * (float(x0) + fiota((nx, 128), 0))
        row_y = 2.0 * (float(y0) + fiota((ny, 128), 0))
        for c in range(CAP):
            spread.append(spread_chunk(floor, above, low, high, c, layer_ids))
            column_weights = [
                jnp.where(
                    layer_ids[:page] == tall(key, c, page), jnp.ones((), BF16), jnp.zeros((), BF16)
                )
                for key in keys
            ]
            wx = hat(x[c : c + 1] - plane_x, 0.5, 0.25)
            wy = hat(y[c : c + 1] - row_y, 0.5, 0.25)
            product = (wx[:, None, :] * wy[None]).reshape(nx * ny, 128)
            weights.append(jnp.concatenate(column_weights + [product.astype(BF16)], axis=0))
        got = mm_nt(jnp.concatenate(weights, axis=1), jnp.concatenate(spread, axis=1))
        if keys:
            _, fnx, _, fny = FINE[dx, dy]
            px = {0: 4, -1: 0, 1: 20}[dx]
            py = {0: 8, -1: 0, 1: 40}[dy]
            fine[px : px + fnx, py : py + fny, :] = got[:fine_rows].reshape(fnx, fny, CZ)
        got = got[fine_rows:].reshape(nx, ny, CZ)[:nx_keep]
        new_x = {0: (0, 9), -1: (0, 4), 1: (1, 5)}[dx] if dy == 0 else (0, 0)
        if (dx, dy) == (0, -1):
            mid[4:13, 0:8, :] = got[:, :8]
            mid[4:13, 8:16, :] += got[:, 8:]
            continue
        for i in range(nx_keep):
            at = (x0 + 4 + i, slice(y0 + 8, y0 + 8 + ny))
            if new_x[0] <= i < new_x[1]:
                mid[at[0], at[1], :] = got[i]
            else:
                mid[at[0], at[1], :] += got[i]

    own = mid[4:13, 8:32, :]
    lateral = bands_ref[1, 0] * own
    for k in range(1, BANDS + 1):
        lateral += bands_ref[1, k] * (
            (mid[4 + k : 13 + k, 8:32, :] + mid[4 - k : 13 - k, 8:32, :])
            + (mid[4:13, 8 + k : 32 + k, :] + mid[4:13, 8 - k : 32 - k, :])
        )
    side_top, side_low = halves(lateral.reshape(216, CZ))
    own_top, own_low = halves(own.reshape(216, CZ))
    coarse = mm(
        jnp.concatenate([side_top, side_low, own_top, own_low, own_top], axis=1),
        jnp.concatenate([g1[...], g1[...], g2t[...], g2t[...], g2l[...]], axis=0),
    )
    coarse = jnp.concatenate([coarse, jnp.zeros((CZ - 216, CZ + 128), F32)], axis=0)
    coarse_top, coarse_low = halves(coarse)
    inner[...] = jnp.concatenate([coarse_top[:, :CZ], coarse_low[:, :CZ]], axis=0)
    field_top, field_low = halves(fine[4:20, 8:40, :].reshape(CX * CY, CZ))
    slab[...] = mm(
        jnp.concatenate([l1[...], l1[...], field_top, field_low, field_top], axis=1),
        jnp.concatenate(
            [coarse_top[:, CZ:], coarse_low[:, CZ:], g0t[:, CZ:], g0t[:, CZ:], g0l[:, CZ:]], axis=0
        ),
    )


def base_kernel(bands_ref, fine, inner, g0t, g0l, l1, base):
    field_top, field_low = halves(fine[4:20, 8:40, :].reshape(CX * CY, CZ))
    base[...] = mm(
        jnp.concatenate([l1[...], l1[...], field_top, field_low, field_top], axis=1),
        jnp.concatenate([inner[...], g0t[:, :CZ], g0t[:, :CZ], g0l[:, :CZ]], axis=0),
    )
    for p in range(CX):
        lateral = jnp.zeros((CY, CZ), F32)
        for k in range(1, BANDS + 1):
            lateral += bands_ref[0, k] * (
                (fine[p + 4 + k, 8:40, :] + fine[p + 4 - k, 8:40, :])
                + (fine[p + 4, 8 + k : 40 + k, :] + fine[p + 4, 8 - k : 40 - k, :])
            )
        base[p * CY : (p + 1) * CY, :] += lateral


def last_kernel(where_ref, gathered, base, slab, table, cx, pz, l2, grid, atoms):
    gz = where_ref[1]
    is_upper = gz == 1
    mine = gathered[pl.ds(16 * gz, 16), :, :].reshape(16 * MSG, 128)
    other = gathered[pl.ds(16 - 16 * gz, 16), :, :].reshape(16 * MSG, 128)

    def conv(table, v):
        top, low = halves(v)
        return mm(table, jnp.concatenate([top, top, low], axis=0))

    values = conv(cx[...], mine)
    across = conv(cx[6 * CX :, :], other)
    lane = iota((CX, 128), 1)
    ninth = values[4 * CX : 5 * CX] + pltpu.roll(values[5 * CX : 6 * CX], 64, 1)
    stacked = jnp.concatenate([values[: 4 * CX], jnp.where(lane < 64, ninth, 0.0)], axis=0)
    shared = jnp.zeros((CX, 128), F32)
    for b in range(PLANES):
        mix = jnp.where(is_upper, 0.0, values[(6 + b) * CX : (7 + b) * CX])
        mix += across[b * CX : (b + 1) * CX]
        shared += pltpu.roll(mix, 128 - 9 * b, 1) if b else mix
    layered = mm_exact_right(stacked, pz[...])
    out_layer = iota((1, CZ), 1)
    shared_weight = hat((out_layer - CZ * (1 - gz)).astype(F32), 1.0, 0.25)
    rows = []
    for y in range(9):
        part = layered[(y // 2) * 16 : (y // 2) * 16 + 16, (y % 2) * CZ : (y % 2 + 1) * CZ]
        rows.append(part + shared[:, 64 + y : 65 + y] * shared_weight)
    coarse = jnp.concatenate(rows, axis=0)
    near = slab[...]
    low = jnp.where(is_upper, near, 0.0)
    high = jnp.where(is_upper, 0.0, near)
    potential = base[...] + mm(l2[...], jnp.concatenate(halves(coarse), axis=0)) + jnp.concatenate([low, high], axis=1)
    grid[...] = potential.reshape(CX, CY, CZ)
    turned = potential.T.astype(BF16)
    _, height, column = atom_rows(table, OWN, 0, CAP)
    layer_ids = fiota((CZ, 128), 0)
    row_ids = layer_ids.astype(BF16)
    keys = fine_key(0, 0, column, None, None)
    for c in range(0, CAP, 2):
        one = [
            jnp.concatenate(
                [
                    jnp.where(row_ids == tall(key, d, CZ), jnp.ones((), BF16), jnp.zeros((), BF16))
                    for key in keys
                ],
                axis=0,
            )
            for d in (c, c + 1)
        ]
        read = mm(turned, jnp.concatenate(one, axis=1))
        for i, d in enumerate((c, c + 1)):
            tent = jnp.maximum(0.0, 1.0 - jnp.abs(layer_ids - height[d : d + 1]))
            atoms[d : d + 1, :] = jnp.sum(
                read[:, i * 128 : (i + 1) * 128] * tent, axis=0, keepdims=True
            )


def vmem():
    return pl.BlockSpec(memory_space=pltpu.VMEM)


def smem():
    return pl.BlockSpec(memory_space=pltpu.SMEM)


def shaped(*pairs):
    return tuple(jax.ShapeDtypeStruct(shape, dtype) for shape, dtype in pairs)


PARAMS = pltpu.CompilerParams(vmem_limit_bytes=VMEM_LIMIT)


def local(charges, heights, columns, counts, bands, cycle_kernel):
    place = jnp.stack([lax.axis_index("gx"), lax.axis_index("gz")]).astype(jnp.int32)
    sent = pl.pallas_call(
        pack_kernel,
        in_specs=[pl.BlockSpec(memory_space=pltpu.HBM)] * 4,
        out_specs=vmem(),
        out_shape=jax.ShapeDtypeStruct((SENDERS, 1, FIELDS), F32),
        scratch_shapes=[
            pltpu.VMEM((CAP, SENDERS), F32),
            pltpu.VMEM((CAP, SENDERS), F32),
            pltpu.VMEM((CAP, SENDERS), jnp.int32),
            pltpu.VMEM((1, SENDERS), jnp.int32),
            pltpu.SemaphoreType.DMA((4,)),
        ],
        name="pack",
    )(charges[0, 0].T, heights[0, 0].T, columns[0, 0].T, counts[0])
    arrived = lax.all_to_all(sent, ("gx", "gy"), split_axis=0, concat_axis=0, tiled=True)
    wide = CZ + 128
    g0t, g0l, g1, g2t, g2l, l1, l2, cx, pz = pl.pallas_call(
        tables_kernel,
        in_specs=[smem(), smem(), smem()],
        out_specs=[vmem()] * 9,
        out_shape=shaped(
            ((CZ, wide), BF16),
            ((CZ, wide), BF16),
            ((CZ, wide), BF16),
            ((CZ, wide), BF16),
            ((CZ, wide), BF16),
            ((CX * CY, CZ), BF16),
            ((CX * CY, 2 * 9 * CX), BF16),
            ((TABLE_ROWS, 3 * 16 * MSG), BF16),
            ((128, 2 * CZ), BF16),
        ),
        compiler_params=PARAMS,
        name="tables",
    )(place, bands, cycle_kernel)
    arrived, g0t, g0l, g1, g2t, g2l, l1, l2, cx, pz = lax.optimization_barrier(
        (arrived, g0t, g0l, g1, g2t, g2l, l1, l2, cx, pz)
    )
    table, message = pl.pallas_call(
        coarse_kernel,
        in_specs=[smem(), vmem()],
        out_specs=[vmem()] * 2,
        out_shape=shaped(((FIELDS, 128), F32), ((32, MSG, 128), F32)),
        compiler_params=PARAMS,
        name="coarse",
    )(place, arrived)
    gathered = lax.all_to_all(message, ("gz", "gx"), split_axis=0, concat_axis=0, tiled=True)
    slab, fine, inner = pl.pallas_call(
        local_kernel,
        in_specs=[smem()] + [vmem()] * 7,
        out_specs=[vmem()] * 3,
        out_shape=shaped(
            ((CX * CY, 128), F32),
            ((CX + 2 * BANDS, CY + 16, CZ), F32),
            ((2 * CZ, CZ), BF16),
        ),
        scratch_shapes=[
            pltpu.VMEM((17, 40, CZ), F32),
        ],
        compiler_params=PARAMS,
        name="local",
    )(bands, table, g0t, g0l, g1, g2t, g2l, l1)
    slab = lax.ppermute(slab, "gz", [(0, 1), (1, 0)])
    base = pl.pallas_call(
        base_kernel,
        in_specs=[smem()] + [vmem()] * 5,
        out_specs=vmem(),
        out_shape=jax.ShapeDtypeStruct((CX * CY, CZ), F32),
        compiler_params=PARAMS,
        cost_estimate=pl.CostEstimate(flops=10**9, bytes_accessed=4 * 10**6, transcendentals=0),
        name="base",
    )(bands, fine, inner, g0t, g0l, l1)
    grid, atoms = pl.pallas_call(
        last_kernel,
        in_specs=[smem()] + [vmem()] * 7,
        out_specs=[vmem()] * 2,
        out_shape=shaped(((CX, CY, CZ), F32), ((CAP, SENDERS), F32)),
        compiler_params=PARAMS,
        name="last",
    )(place, gathered, base, slab, table, cx, pz, l2)
    return grid, atoms.T[None, None]


def solution(mesh):
    placed = (
        P("gz", ("gx", "gy"), None, None),
        P("gz", ("gx", "gy"), None, None),
        P("gz", ("gx", "gy"), None, None),
        P("gz", ("gx", "gy"), None),
        P(),
        P(),
    )
    return jax.shard_map(
        local,
        mesh=mesh,
        in_specs=placed,
        out_specs=(P("gx", "gy", "gz"), P("gz", ("gx", "gy"), None, None)),
        check_vma=False,
    )
```

```python
import jax
import jax.numpy as jnp
from jax import lax
from jax.experimental import pallas as pl
from jax.experimental.pallas import tpu as pltpu
from jax.sharding import PartitionSpec as P

CX, CY, CZ, CAP = 16, 32, 256, 16
BANDS = 4
SENDERS = 128
NEAR = 3 * CAP
FIELDS = 9 * NEAR
PLANES = 5
MSG = 24
FOLDED = 4 * PLANES
TABLE_ROWS = (4 + 2 + PLANES) * CX
F32, BF16 = jnp.float32, jnp.bfloat16
HIGH = lax.Precision.HIGHEST
VMEM_LIMIT = 48 * 1024 * 1024

OWN = 4
REACH = {
    (0, 0): (0, 9, 10, 0, 24),
    (-1, 0): (-4, 5, 6, 0, 24),
    (1, 0): (8, 5, 6, 0, 24),
    (0, -1): (0, 9, 9, -8, 16),
    (0, 1): (0, 9, 10, 16, 8),
    (-1, -1): (-4, 5, 5, -8, 16),
    (-1, 1): (-4, 5, 6, 16, 8),
    (1, -1): (8, 5, 5, -8, 16),
    (1, 1): (8, 5, 6, 16, 8),
}
FINE = {
    (0, 0): (0, 16, 0, 32),
    (-1, 0): (12, 4, 0, 32),
    (1, 0): (0, 4, 0, 32),
    (0, -1): (0, 16, 24, 8),
    (0, 1): (0, 16, 0, 8),
}


def iota(shape, dim):
    return lax.broadcasted_iota(jnp.int32, shape, dim)


def fiota(shape, dim):
    return iota(shape, dim).astype(F32)


def hat(distance, peak, slope):
    return jnp.maximum(0.0, peak - slope * jnp.abs(distance))


def mm(a, b):
    return lax.dot_general(a, b, (((1,), (0,)), ((), ())), preferred_element_type=F32)


def mm_nt(a, b):
    return lax.dot_general(a, b, (((1,), (1,)), ((), ())), preferred_element_type=F32)


def halves(a):
    top = a.astype(BF16)
    return top, (a - top.astype(F32)).astype(BF16)


def mm_exact_right(a, b):
    return mm(jnp.concatenate(halves(a), axis=1), jnp.concatenate([b, b], axis=0))


def mm_exact_left(a, b):
    return mm(jnp.concatenate([a, a], axis=1), jnp.concatenate(halves(b), axis=0))


def block_index(dx, dy):
    return (dx + 1) * 3 + dy + 1


def atom_rows(table, block, first, count):
    base = block * NEAR + first
    return (
        table[pl.ds(base, count), :],
        table[pl.ds(base + CAP, count), :],
        table[pl.ds(base + 2 * CAP, count), :],
    )


def tent_rows(charge, height):
    floor = jnp.floor(height)
    above = floor + 1.0
    low = charge * jnp.maximum(0.0, 1.0 - jnp.abs(floor - height))
    high = charge * jnp.maximum(0.0, 1.0 - jnp.abs(above - height))
    return floor, above, low, high


def tall(rows, c, count):
    one = jnp.broadcast_to(rows[c : c + 1], (16, 128)).astype(BF16)
    return jnp.concatenate([one] * (count // 16), axis=0)


def spread_chunk(floor, above, low, high, c, layer_ids):
    rest = jnp.where(layer_ids == tall(above, c, CZ), tall(high, c, CZ), jnp.zeros((), BF16))
    return jnp.where(layer_ids == tall(floor, c, CZ), tall(low, c, CZ), rest)


def place_of(column):
    x = jnp.floor(column * (1.0 / CY))
    return x, column - CY * x


def tables_kernel(where_ref, bands_ref, cycle_ref, g0t, g0l, g1, g2t, g2l, l1, l2, cx, pz):
    gx, gz = where_ref[0], where_ref[1]
    wide = CZ + 128
    shape = (CZ, wide)
    row = iota(shape, 0)
    lane = iota(shape, 1)
    first = CZ * gz
    out_layer = jnp.where(lane < CZ, first + lane, lane - (128 * gz))
    step = jnp.abs(first + row - out_layer)
    zero = jnp.zeros(shape, F32)
    total = jnp.where(step == 0, bands_ref[0, 0], zero)
    for k in range(1, BANDS + 1):
        total = jnp.where(step == k, bands_ref[0, k], total)
    g0t[...], g0l[...] = halves(total)
    square = (CZ, CZ)
    down = hat((first + iota(square, 0) - 2 * iota(square, 1)).astype(F32), 0.5, 0.25)
    up_out = jnp.where(lane < CZ, first + lane, lane - (128 * gz))
    up = hat((up_out - 2 * row).astype(F32), 1.0, 0.5)
    g1[...] = mm(down.astype(BF16), up.astype(BF16)).astype(BF16)
    step1 = jnp.abs(iota(square, 0) - iota(square, 1))
    total1 = jnp.zeros(square, F32)
    for k in range(1, BANDS + 1):
        total1 = jnp.where(step1 == k, bands_ref[1, k], total1)
    middle = mm_exact_left(down.astype(BF16), total1)
    g2t[...], g2l[...] = halves(mm_exact_right(middle, up.astype(BF16)))
    s1 = (CX * CY, CZ)
    cell, coarse = iota(s1, 0), iota(s1, 1)
    product = hat((cell // CY - 2 * (coarse // 24)).astype(F32), 1.0, 0.5) * hat(
        (cell % CY - 2 * (coarse % 24)).astype(F32), 1.0, 0.5
    )
    l1[...] = jnp.where(coarse < 9 * 24, product, 0.0).astype(BF16)
    s2 = (CX * CY, 2 * 9 * CX)
    cell, coarse = iota(s2, 0), iota(s2, 1) % (9 * CX)
    l2[...] = jnp.where(
        cell // CY == coarse % CX,
        hat((cell % CY - 4 * (coarse // CX)).astype(F32), 1.0, 0.25),
        0.0,
    ).astype(BF16)
    s3 = (8, 16 * MSG)
    a, source = iota(s3, 0), iota(s3, 1)
    s4 = (CX, 8)
    px = hat((iota(s4, 0) - 4 * iota(s4, 1)).astype(F32), 1.0, 0.25)
    row = source % MSG
    late = 2 * (row - FOLDED)

    def circulant(plane):
        offset = (4 * (gx - source // MSG) + a - plane + 128) % 64
        picked = jnp.zeros(s3, F32)
        for o in range(64):
            picked = jnp.where(offset == o, cycle_ref[o], picked)
        return lax.dot_general(
            px, picked, (((1,), (0,)), ((), ())), preferred_element_type=F32, precision=HIGH
        )

    even = circulant(jnp.where(row < FOLDED, row % PLANES, late))
    odd = circulant(late + 1)
    at = iota((CX, 16 * MSG), 1) % MSG
    pieces = [jnp.where(at // PLANES == t, even, 0.0) for t in range(4)]
    pieces.append(jnp.where((at >= FOLDED) & (at < FOLDED + 3), even, 0.0))
    pieces.append(jnp.where((at >= FOLDED) & (at < FOLDED + 2), odd, 0.0))
    for b in range(PLANES):
        pieces.append(jnp.where(at == FOLDED + 2, circulant(b), 0.0))
    count = 16 * MSG
    for i, piece in enumerate(pieces):
        top, low = halves(piece)
        rows = slice(i * CX, (i + 1) * CX)
        cx[rows, 0:count] = top
        cx[rows, count : 2 * count] = low
        cx[rows, 2 * count :] = top
    s5 = (128, 2 * CZ)
    z, out = iota(s5, 0), iota(s5, 1)
    weight = hat((out % CZ - 4 * (z % 64)).astype(F32), 1.0, 0.25)
    pz[...] = jnp.where((z < 64) == (out < CZ), weight, 0.0).astype(BF16)


def pack_kernel(charges_in, heights_in, columns_in, counts_in, message, charges, heights, columns, counts, done):
    pairs = ((counts_in, counts), (charges_in, charges), (columns_in, columns), (heights_in, heights))
    copies = [pltpu.make_async_copy(a, b, done.at[i]) for i, (a, b) in enumerate(pairs)]
    for copy in copies:
        copy.start()
    for copy in copies:
        copy.wait()
    live = iota((CAP, SENDERS), 0) < counts[...]
    own = jnp.concatenate(
        [
            jnp.where(live, charges[...], 0.0),
            heights[...],
            jnp.where(live, columns[...].astype(F32), -1.0),
        ],
        axis=0,
    )
    ring = iota((NEAR, SENDERS), 1) % 8
    below = jnp.where(ring == 0, pltpu.roll(own, SENDERS - 7, 1), pltpu.roll(own, 1, 1))
    above = jnp.where(ring == 7, pltpu.roll(own, 7, 1), pltpu.roll(own, SENDERS - 1, 1))
    near = []
    for turn in (8, 0, SENDERS - 8):
        for part in (below, own, above):
            near.append(pltpu.roll(part, turn, 1) if turn else part)
    table = jnp.concatenate(near, axis=0)
    for i in range(0, FIELDS, 128):
        at = slice(i, min(i + 128, FIELDS))
        message[:, 0, at] = table[at, :].T


def coarse_kernel(where_ref, arrived, table, message):
    gz = where_ref[1]
    for i in range(0, FIELDS, 128):
        at = slice(i, min(i + 128, FIELDS))
        table[at, :] = arrived[:, 0, at].T
    layer_ids = fiota((CZ, 128), 0).astype(BF16)
    cell_x = 4.0 * fiota((8, 128), 0)
    cell_y = 4.0 * fiota((10, 128), 0)
    spread, weights = [], []
    for dy in (-1, 0, 1):
        charge, height, column = atom_rows(table, block_index(0, dy), 0, CAP)
        floor, above, low, high = tent_rows(charge, height)
        x, y = place_of(column)
        y = y + float(CY * dy)
        for c in range(CAP):
            spread.append(spread_chunk(floor, above, low, high, c, layer_ids))
            wx = hat(x[c : c + 1] - cell_x, 0.25, 0.0625)
            wy = hat(y[c : c + 1] - cell_y, 0.25, 0.0625)
            weights.append((wy[:, None, :] * wx[None]).reshape(80, 128).astype(BF16))
    lateral = mm_nt(jnp.concatenate(weights, axis=1), jnp.concatenate(spread, axis=1))
    layer, out = iota((CZ, 128), 0), iota((CZ, 128), 1)
    down = hat((layer - jnp.where(out < 64, 4 * out, CZ * (1 - gz))).astype(F32), 0.25, 0.0625)
    coarse = mm_exact_right(lateral, down.astype(BF16))
    lane = iota((8, 128), 1)
    tiles = [coarse[8 * y : 8 * y + 8, :] for y in range(9)]
    parts = [
        jnp.where(lane < 64, tiles[2 * t], pltpu.roll(tiles[2 * t + 1], 64, 1)) for t in range(4)
    ]
    shared = jnp.zeros((8, 128), F32)
    for y in range(9):
        shared = jnp.where(lane == 64 + y, pltpu.roll(tiles[y], y, 1) if y else tiles[y], shared)
    turned = pltpu.roll(tiles[8], 64, 1)
    row = lane[:1]
    beside = jnp.zeros((1, 128), F32)
    for b in range(PLANES):
        moved = pltpu.roll(shared, 9 * b, 1) if b else shared
        beside = jnp.where((row >= 64 + 9 * b) & (row < 73 + 9 * b), moved[b : b + 1], beside)
    folded = [
        jnp.where(row < 64, tiles[8][0:1], turned[1:2]),
        jnp.where(row < 64, tiles[8][2:3], turned[3:4]),
        jnp.where(row < 64, tiles[8][4:5], beside),
        jnp.zeros((1, 128), F32),
    ]
    packed = jnp.concatenate([part[:PLANES] for part in parts] + folded, axis=0)
    for s in range(16):
        message[s] = packed


def fine_key(dx, dy, column, x, y):
    if dx:
        return [column - float(CX * CY - 128) if dx < 0 else column]
    if dy:
        local_y = y - float(CY - 8) if dy < 0 else y
        inside = (local_y >= 0.0) & (local_y < 8.0)
        return [jnp.where(inside, 8.0 * x + local_y, -1.0)]
    return [column, column - 256.0]


def local_kernel(bands_ref, table, g0t, g0l, g1, g2t, g2l, l1, slab, fine, inner, mid):
    layer_ids = fiota((CZ, 128), 0).astype(BF16)
    mid[4:13, 32:40, :] = jnp.zeros((9, 8, CZ), F32)
    order = [(0, 0), (-1, 0), (1, 0), (0, -1), (0, 1), (-1, -1), (-1, 1), (1, -1), (1, 1)]
    for n, (dx, dy) in enumerate(order):
        spread, weights = [], []
        charge, height, column = atom_rows(table, block_index(dx, dy), 0, CAP)
        floor, above, low, high = tent_rows(charge, height)
        x, y = place_of(column)
        keys = fine_key(dx, dy, column, x, y) if (dx, dy) in FINE else []
        x = x + float(CX * dx)
        y = y + float(CY * dy)
        x0, nx_keep, nx, y0, ny = REACH[dx, dy]
        page = CZ if (dx, dy) == (0, 0) else 128
        fine_rows = page * len(keys)
        plane_x = 2.0 * (float(x0) + fiota((nx, 128), 0))
        row_y = 2.0 * (float(y0) + fiota((ny, 128), 0))
        for c in range(CAP):
            spread.append(spread_chunk(floor, above, low, high, c, layer_ids))
            column_weights = [
                jnp.where(
                    layer_ids[:page] == tall(key, c, page), jnp.ones((), BF16), jnp.zeros((), BF16)
                )
                for key in keys
            ]
            wx = hat(x[c : c + 1] - plane_x, 0.5, 0.25)
            wy = hat(y[c : c + 1] - row_y, 0.5, 0.25)
            product = (wx[:, None, :] * wy[None]).reshape(nx * ny, 128)
            weights.append(jnp.concatenate(column_weights + [product.astype(BF16)], axis=0))
        got = mm_nt(jnp.concatenate(weights, axis=1), jnp.concatenate(spread, axis=1))
        if keys:
            _, fnx, _, fny = FINE[dx, dy]
            px = {0: 4, -1: 0, 1: 20}[dx]
            py = {0: 8, -1: 0, 1: 40}[dy]
            fine[px : px + fnx, py : py + fny, :] = got[:fine_rows].reshape(fnx, fny, CZ)
        got = got[fine_rows:].reshape(nx, ny, CZ)[:nx_keep]
        new_x = {0: (0, 9), -1: (0, 4), 1: (1, 5)}[dx] if dy == 0 else (0, 0)
        if (dx, dy) == (0, -1):
            mid[4:13, 0:8, :] = got[:, :8]
            mid[4:13, 8:16, :] += got[:, 8:]
            continue
        for i in range(nx_keep):
            at = (x0 + 4 + i, slice(y0 + 8, y0 + 8 + ny))
            if new_x[0] <= i < new_x[1]:
                mid[at[0], at[1], :] = got[i]
            else:
                mid[at[0], at[1], :] += got[i]

    own = mid[4:13, 8:32, :]
    lateral = bands_ref[1, 0] * own
    for k in range(1, BANDS + 1):
        lateral += bands_ref[1, k] * (
            (mid[4 + k : 13 + k, 8:32, :] + mid[4 - k : 13 - k, 8:32, :])
            + (mid[4:13, 8 + k : 32 + k, :] + mid[4:13, 8 - k : 32 - k, :])
        )
    side_top, side_low = halves(lateral.reshape(216, CZ))
    own_top, own_low = halves(own.reshape(216, CZ))
    coarse = mm(
        jnp.concatenate([side_top, side_low, own_top, own_low, own_top], axis=1),
        jnp.concatenate([g1[...], g1[...], g2t[...], g2t[...], g2l[...]], axis=0),
    )
    coarse = jnp.concatenate([coarse, jnp.zeros((CZ - 216, CZ + 128), F32)], axis=0)
    coarse_top, coarse_low = halves(coarse)
    inner[...] = jnp.concatenate([coarse_top[:, :CZ], coarse_low[:, :CZ]], axis=0)
    field_top, field_low = halves(fine[4:20, 8:40, :].reshape(CX * CY, CZ))
    slab[...] = mm(
        jnp.concatenate([l1[...], l1[...], field_top, field_low, field_top], axis=1),
        jnp.concatenate(
            [coarse_top[:, CZ:], coarse_low[:, CZ:], g0t[:, CZ:], g0t[:, CZ:], g0l[:, CZ:]], axis=0
        ),
    )


def base_kernel(bands_ref, fine, inner, g0t, g0l, l1, base):
    field_top, field_low = halves(fine[4:20, 8:40, :].reshape(CX * CY, CZ))
    base[...] = mm(
        jnp.concatenate([l1[...], l1[...], field_top, field_low, field_top], axis=1),
        jnp.concatenate([inner[...], g0t[:, :CZ], g0t[:, :CZ], g0l[:, :CZ]], axis=0),
    )
    for p in range(CX):
        lateral = jnp.zeros((CY, CZ), F32)
        for k in range(1, BANDS + 1):
            lateral += bands_ref[0, k] * (
                (fine[p + 4 + k, 8:40, :] + fine[p + 4 - k, 8:40, :])
                + (fine[p + 4, 8 + k : 40 + k, :] + fine[p + 4, 8 - k : 40 - k, :])
            )
        base[p * CY : (p + 1) * CY, :] += lateral


def circulant_kernel(gathered, cx, chunks, shared):
    top, low = halves(gathered[...].reshape(16 * MSG, 128))
    values = mm(cx[...], jnp.concatenate([top, top, low], axis=0))
    total = values[6 * CX : 7 * CX]
    for b in range(1, PLANES):
        total += pltpu.roll(values[(6 + b) * CX : (7 + b) * CX], 128 - 9 * b, 1)
    shared[...] = total
    lane = iota((CX, 128), 1)
    ninth = values[4 * CX : 5 * CX] + pltpu.roll(values[5 * CX : 6 * CX], 64, 1)
    chunks[...] = jnp.concatenate([values[: 4 * CX], jnp.where(lane < 64, ninth, 0.0)], axis=0)


def lift_kernel(where_ref, chunks, shared, base, pz, l2, partial):
    gz = where_ref[1]
    is_upper = gz == 1
    layered = mm_exact_right(chunks[...], pz[...])
    own = jnp.where(is_upper, 0.0, shared[...])
    weight = hat((iota((1, CZ), 1) - CZ).astype(F32), 1.0, 0.25)
    rows = []
    for y in range(9):
        part = layered[(y // 2) * 16 : (y // 2) * 16 + 16, (y % 2) * CZ : (y % 2 + 1) * CZ]
        rows.append(part + own[:, 64 + y : 65 + y] * weight)
    coarse = jnp.concatenate(rows, axis=0)
    partial[...] = base[...] + mm(l2[...], jnp.concatenate(halves(coarse), axis=0))


def read_kernel(where_ref, partial, across, slab, l2, table, grid, atoms):
    gz = where_ref[1]
    is_upper = gz == 1
    weight = hat((iota((1, 128), 1) - 128 * (1 - gz)).astype(F32), 1.0, 0.25)
    rows = [across[:, 64 + y : 65 + y] * weight for y in range(9)]
    near = slab[...] + mm(l2[...], jnp.concatenate(halves(jnp.concatenate(rows, axis=0)), axis=0))
    low = jnp.where(is_upper, near, 0.0)
    high = jnp.where(is_upper, 0.0, near)
    potential = partial[...] + jnp.concatenate([low, high], axis=1)
    grid[...] = potential.reshape(CX, CY, CZ)
    turned = potential.T.astype(BF16)
    _, height, column = atom_rows(table, OWN, 0, CAP)
    layer_ids = fiota((CZ, 128), 0)
    row_ids = layer_ids.astype(BF16)
    keys = fine_key(0, 0, column, None, None)
    for c in range(0, CAP, 2):
        one = [
            jnp.concatenate(
                [
                    jnp.where(row_ids == tall(key, d, CZ), jnp.ones((), BF16), jnp.zeros((), BF16))
                    for key in keys
                ],
                axis=0,
            )
            for d in (c, c + 1)
        ]
        read = mm(turned, jnp.concatenate(one, axis=1))
        for i, d in enumerate((c, c + 1)):
            tent = jnp.maximum(0.0, 1.0 - jnp.abs(layer_ids - height[d : d + 1]))
            atoms[d : d + 1, :] = jnp.sum(
                read[:, i * 128 : (i + 1) * 128] * tent, axis=0, keepdims=True
            )


def vmem():
    return pl.BlockSpec(memory_space=pltpu.VMEM)


def smem():
    return pl.BlockSpec(memory_space=pltpu.SMEM)


def shaped(*pairs):
    return tuple(jax.ShapeDtypeStruct(shape, dtype) for shape, dtype in pairs)


PARAMS = pltpu.CompilerParams(vmem_limit_bytes=VMEM_LIMIT)


def local(charges, heights, columns, counts, bands, cycle_kernel):
    place = jnp.stack([lax.axis_index("gx"), lax.axis_index("gz")]).astype(jnp.int32)
    sent = pl.pallas_call(
        pack_kernel,
        in_specs=[pl.BlockSpec(memory_space=pltpu.HBM)] * 4,
        out_specs=vmem(),
        out_shape=jax.ShapeDtypeStruct((SENDERS, 1, FIELDS), F32),
        scratch_shapes=[
            pltpu.VMEM((CAP, SENDERS), F32),
            pltpu.VMEM((CAP, SENDERS), F32),
            pltpu.VMEM((CAP, SENDERS), jnp.int32),
            pltpu.VMEM((1, SENDERS), jnp.int32),
            pltpu.SemaphoreType.DMA((4,)),
        ],
        name="pack",
    )(charges[0, 0].T, heights[0, 0].T, columns[0, 0].T, counts[0])
    arrived = lax.all_to_all(sent, ("gx", "gy"), split_axis=0, concat_axis=0, tiled=True)
    wide = CZ + 128
    g0t, g0l, g1, g2t, g2l, l1, l2, cx, pz = pl.pallas_call(
        tables_kernel,
        in_specs=[smem(), smem(), smem()],
        out_specs=[vmem()] * 9,
        out_shape=shaped(
            ((CZ, wide), BF16),
            ((CZ, wide), BF16),
            ((CZ, wide), BF16),
            ((CZ, wide), BF16),
            ((CZ, wide), BF16),
            ((CX * CY, CZ), BF16),
            ((CX * CY, 2 * 9 * CX), BF16),
            ((TABLE_ROWS, 3 * 16 * MSG), BF16),
            ((128, 2 * CZ), BF16),
        ),
        compiler_params=PARAMS,
        name="tables",
    )(place, bands, cycle_kernel)
    arrived, g0t, g0l, g1, g2t, g2l, l1, l2, cx, pz = lax.optimization_barrier(
        (arrived, g0t, g0l, g1, g2t, g2l, l1, l2, cx, pz)
    )
    table, message = pl.pallas_call(
        coarse_kernel,
        in_specs=[smem(), vmem()],
        out_specs=[vmem()] * 2,
        out_shape=shaped(((FIELDS, 128), F32), ((16, MSG, 128), F32)),
        compiler_params=PARAMS,
        name="coarse",
    )(place, arrived)
    gathered = lax.all_to_all(message, "gx", split_axis=0, concat_axis=0, tiled=True)
    slab, fine, inner = pl.pallas_call(
        local_kernel,
        in_specs=[smem()] + [vmem()] * 7,
        out_specs=[vmem()] * 3,
        out_shape=shaped(
            ((CX * CY, 128), F32),
            ((CX + 2 * BANDS, CY + 16, CZ), F32),
            ((2 * CZ, CZ), BF16),
        ),
        scratch_shapes=[
            pltpu.VMEM((17, 40, CZ), F32),
        ],
        compiler_params=PARAMS,
        name="local",
    )(bands, table, g0t, g0l, g1, g2t, g2l, l1)
    base = pl.pallas_call(
        base_kernel,
        in_specs=[smem()] + [vmem()] * 5,
        out_specs=vmem(),
        out_shape=jax.ShapeDtypeStruct((CX * CY, CZ), F32),
        compiler_params=PARAMS,
        cost_estimate=pl.CostEstimate(flops=10**9, bytes_accessed=4 * 10**6, transcendentals=0),
        name="base",
    )(bands, fine, inner, g0t, g0l, l1)
    gathered, slab, base = lax.optimization_barrier((gathered, slab, base))
    slab = lax.ppermute(slab, "gz", [(0, 1), (1, 0)])
    chunks, shared = pl.pallas_call(
        circulant_kernel,
        in_specs=[vmem()] * 2,
        out_specs=[vmem()] * 2,
        out_shape=shaped(((5 * CX, 128), F32), ((CX, 128), F32)),
        compiler_params=PARAMS,
        name="circulant",
    )(gathered, cx)
    across = lax.ppermute(shared, "gz", [(0, 1), (1, 0)])
    partial = pl.pallas_call(
        lift_kernel,
        in_specs=[smem()] + [vmem()] * 5,
        out_specs=vmem(),
        out_shape=jax.ShapeDtypeStruct((CX * CY, CZ), F32),
        compiler_params=PARAMS,
        cost_estimate=pl.CostEstimate(flops=10**9, bytes_accessed=4 * 10**6, transcendentals=0),
        name="lift",
    )(place, chunks, shared, base, pz, l2)
    grid, atoms = pl.pallas_call(
        read_kernel,
        in_specs=[smem()] + [vmem()] * 5,
        out_specs=[vmem()] * 2,
        out_shape=shaped(((CX, CY, CZ), F32), ((CAP, SENDERS), F32)),
        compiler_params=PARAMS,
        name="read",
    )(place, partial, across, slab, l2, table)
    return grid, atoms.T[None, None]


def solution(mesh):
    placed = (
        P("gz", ("gx", "gy"), None, None),
        P("gz", ("gx", "gy"), None, None),
        P("gz", ("gx", "gy"), None, None),
        P("gz", ("gx", "gy"), None),
        P(),
        P(),
    )
    return jax.shard_map(
        local,
        mesh=mesh,
        in_specs=placed,
        out_specs=(P("gx", "gy", "gz"), P("gz", ("gx", "gy"), None, None)),
        check_vma=False,
    )
```

```python
import jax
import jax.numpy as jnp
from jax import lax
from jax.experimental import pallas as pl
from jax.experimental.pallas import tpu as pltpu
from jax.sharding import PartitionSpec as P

CX, CY, CZ, CAP = 16, 32, 256, 16
BANDS = 4
SENDERS = 128
NEAR = 3 * CAP
FIELDS = 9 * NEAR
PLANES = 5
MSG = 24
FOLDED = 4 * PLANES
TABLE_ROWS = (4 + 2 + PLANES) * CX
F32, BF16 = jnp.float32, jnp.bfloat16
HIGH = lax.Precision.HIGHEST
VMEM_LIMIT = 48 * 1024 * 1024

OWN = 4
REACH = {
    (0, 0): (0, 9, 10, 0, 24),
    (-1, 0): (-4, 5, 6, 0, 24),
    (1, 0): (8, 5, 6, 0, 24),
    (0, -1): (0, 9, 9, -8, 16),
    (0, 1): (0, 9, 10, 16, 8),
    (-1, -1): (-4, 5, 5, -8, 16),
    (-1, 1): (-4, 5, 6, 16, 8),
    (1, -1): (8, 5, 5, -8, 16),
    (1, 1): (8, 5, 6, 16, 8),
}
FINE = {
    (0, 0): (0, 16, 0, 32),
    (-1, 0): (12, 4, 0, 32),
    (1, 0): (0, 4, 0, 32),
    (0, -1): (0, 16, 24, 8),
    (0, 1): (0, 16, 0, 8),
}


def iota(shape, dim):
    return lax.broadcasted_iota(jnp.int32, shape, dim)


def fiota(shape, dim):
    return iota(shape, dim).astype(F32)


def hat(distance, peak, slope):
    return jnp.maximum(0.0, peak - slope * jnp.abs(distance))


def mm(a, b):
    return lax.dot_general(a, b, (((1,), (0,)), ((), ())), preferred_element_type=F32)


def mm_nt(a, b):
    return lax.dot_general(a, b, (((1,), (1,)), ((), ())), preferred_element_type=F32)


def halves(a):
    top = a.astype(BF16)
    return top, (a - top.astype(F32)).astype(BF16)


def mm_exact_right(a, b):
    return mm(jnp.concatenate(halves(a), axis=1), jnp.concatenate([b, b], axis=0))


def mm_exact_left(a, b):
    return mm(jnp.concatenate([a, a], axis=1), jnp.concatenate(halves(b), axis=0))


def block_index(dx, dy):
    return (dx + 1) * 3 + dy + 1


def atom_rows(table, block, first, count):
    base = block * NEAR + first
    return (
        table[pl.ds(base, count), :],
        table[pl.ds(base + CAP, count), :],
        table[pl.ds(base + 2 * CAP, count), :],
    )


def tent_rows(charge, height):
    floor = jnp.floor(height)
    above = floor + 1.0
    low = charge * jnp.maximum(0.0, 1.0 - jnp.abs(floor - height))
    high = charge * jnp.maximum(0.0, 1.0 - jnp.abs(above - height))
    return floor, above, low, high


def tall(rows, c, count):
    one = jnp.broadcast_to(rows[c : c + 1], (16, 128)).astype(BF16)
    return jnp.concatenate([one] * (count // 16), axis=0)


def spread_chunk(floor, above, low, high, c, layer_ids):
    rest = jnp.where(layer_ids == tall(above, c, CZ), tall(high, c, CZ), jnp.zeros((), BF16))
    return jnp.where(layer_ids == tall(floor, c, CZ), tall(low, c, CZ), rest)


def place_of(column):
    x = jnp.floor(column * (1.0 / CY))
    return x, column - CY * x


def tables_kernel(where_ref, bands_ref, cycle_ref, g0t, g0l, g1, g2t, g2l, l1, l2, cx, pz):
    gx, gz = where_ref[0], where_ref[1]
    wide = CZ + 128
    shape = (CZ, wide)
    row = iota(shape, 0)
    lane = iota(shape, 1)
    first = CZ * gz
    out_layer = jnp.where(lane < CZ, first + lane, lane - (128 * gz))
    step = jnp.abs(first + row - out_layer)
    zero = jnp.zeros(shape, F32)
    total = jnp.where(step == 0, bands_ref[0, 0], zero)
    for k in range(1, BANDS + 1):
        total = jnp.where(step == k, bands_ref[0, k], total)
    g0t[...], g0l[...] = halves(total)
    square = (CZ, CZ)
    down = hat((first + iota(square, 0) - 2 * iota(square, 1)).astype(F32), 0.5, 0.25)
    up_out = jnp.where(lane < CZ, first + lane, lane - (128 * gz))
    up = hat((up_out - 2 * row).astype(F32), 1.0, 0.5)
    g1[...] = mm(down.astype(BF16), up.astype(BF16)).astype(BF16)
    step1 = jnp.abs(iota(square, 0) - iota(square, 1))
    total1 = jnp.zeros(square, F32)
    for k in range(1, BANDS + 1):
        total1 = jnp.where(step1 == k, bands_ref[1, k], total1)
    middle = mm_exact_left(down.astype(BF16), total1)
    g2t[...], g2l[...] = halves(mm_exact_right(middle, up.astype(BF16)))
    s1 = (CX * CY, CZ)
    cell, coarse = iota(s1, 0), iota(s1, 1)
    product = hat((cell // CY - 2 * (coarse // 24)).astype(F32), 1.0, 0.5) * hat(
        (cell % CY - 2 * (coarse % 24)).astype(F32), 1.0, 0.5
    )
    l1[...] = jnp.where(coarse < 9 * 24, product, 0.0).astype(BF16)
    s2 = (CX * CY, 2 * 9 * CX)
    cell, coarse = iota(s2, 0), iota(s2, 1) % (9 * CX)
    l2[...] = jnp.where(
        cell // CY == coarse % CX,
        hat((cell % CY - 4 * (coarse // CX)).astype(F32), 1.0, 0.25),
        0.0,
    ).astype(BF16)
    s3 = (8, 16 * MSG)
    a, source = iota(s3, 0), iota(s3, 1)
    s4 = (CX, 8)
    px = hat((iota(s4, 0) - 4 * iota(s4, 1)).astype(F32), 1.0, 0.25)
    row = source % MSG
    late = 2 * (row - FOLDED)

    def circulant(plane):
        offset = (4 * (gx - source // MSG) + a - plane + 128) % 64
        picked = jnp.zeros(s3, F32)
        for o in range(64):
            picked = jnp.where(offset == o, cycle_ref[o], picked)
        return lax.dot_general(
            px, picked, (((1,), (0,)), ((), ())), preferred_element_type=F32, precision=HIGH
        )

    even = circulant(jnp.where(row < FOLDED, row % PLANES, late))
    odd = circulant(late + 1)
    at = iota((CX, 16 * MSG), 1) % MSG
    pieces = [jnp.where(at // PLANES == t, even, 0.0) for t in range(4)]
    pieces.append(jnp.where((at >= FOLDED) & (at < FOLDED + 3), even, 0.0))
    pieces.append(jnp.where((at >= FOLDED) & (at < FOLDED + 2), odd, 0.0))
    for b in range(PLANES):
        pieces.append(jnp.where(at == FOLDED + 2, circulant(b), 0.0))
    count = 16 * MSG
    for i, piece in enumerate(pieces):
        top, low = halves(piece)
        rows = slice(i * CX, (i + 1) * CX)
        cx[rows, 0:count] = top
        cx[rows, count : 2 * count] = low
        cx[rows, 2 * count :] = top
    s5 = (128, 2 * CZ)
    z, out = iota(s5, 0), iota(s5, 1)
    weight = hat((out % CZ - 4 * (z % 64)).astype(F32), 1.0, 0.25)
    pz[...] = jnp.where((z < 64) == (out < CZ), weight, 0.0).astype(BF16)


def pack_kernel(charges_in, heights_in, columns_in, counts_in, message, charges, heights, columns, counts, done):
    pairs = ((counts_in, counts), (charges_in, charges), (columns_in, columns), (heights_in, heights))
    copies = [pltpu.make_async_copy(a, b, done.at[i]) for i, (a, b) in enumerate(pairs)]
    for copy in copies:
        copy.start()
    for copy in copies:
        copy.wait()
    live = iota((CAP, SENDERS), 0) < counts[...]
    own = jnp.concatenate(
        [
            jnp.where(live, charges[...], 0.0),
            heights[...],
            jnp.where(live, columns[...].astype(F32), -1.0),
        ],
        axis=0,
    )
    ring = iota((NEAR, SENDERS), 1) % 8
    below = jnp.where(ring == 0, pltpu.roll(own, SENDERS - 7, 1), pltpu.roll(own, 1, 1))
    above = jnp.where(ring == 7, pltpu.roll(own, 7, 1), pltpu.roll(own, SENDERS - 1, 1))
    near = []
    for turn in (8, 0, SENDERS - 8):
        for part in (below, own, above):
            near.append(pltpu.roll(part, turn, 1) if turn else part)
    table = jnp.concatenate(near, axis=0)
    for i in range(0, FIELDS, 128):
        at = slice(i, min(i + 128, FIELDS))
        message[:, 0, at] = table[at, :].T


def coarse_kernel(where_ref, arrived, table, message):
    gz = where_ref[1]
    for i in range(0, FIELDS, 128):
        at = slice(i, min(i + 128, FIELDS))
        table[at, :] = arrived[:, 0, at].T
    layer_ids = fiota((CZ, 128), 0).astype(BF16)
    cell_x = 4.0 * fiota((8, 128), 0)
    cell_y = 4.0 * fiota((10, 128), 0)
    spread, weights = [], []
    for dy in (-1, 0, 1):
        charge, height, column = atom_rows(table, block_index(0, dy), 0, CAP)
        floor, above, low, high = tent_rows(charge, height)
        x, y = place_of(column)
        y = y + float(CY * dy)
        for c in range(CAP):
            spread.append(spread_chunk(floor, above, low, high, c, layer_ids))
            wx = hat(x[c : c + 1] - cell_x, 0.25, 0.0625)
            wy = hat(y[c : c + 1] - cell_y, 0.25, 0.0625)
            weights.append((wy[:, None, :] * wx[None]).reshape(80, 128).astype(BF16))
    lateral = mm_nt(jnp.concatenate(weights, axis=1), jnp.concatenate(spread, axis=1))
    layer, out = iota((CZ, 128), 0), iota((CZ, 128), 1)
    down = hat((layer - jnp.where(out < 64, 4 * out, CZ * (1 - gz))).astype(F32), 0.25, 0.0625)
    coarse = mm_exact_right(lateral, down.astype(BF16))
    lane = iota((8, 128), 1)
    tiles = [coarse[8 * y : 8 * y + 8, :] for y in range(9)]
    parts = [
        jnp.where(lane < 64, tiles[2 * t], pltpu.roll(tiles[2 * t + 1], 64, 1)) for t in range(4)
    ]
    shared = jnp.zeros((8, 128), F32)
    for y in range(9):
        shared = jnp.where(lane == 64 + y, pltpu.roll(tiles[y], y, 1) if y else tiles[y], shared)
    turned = pltpu.roll(tiles[8], 64, 1)
    row = lane[:1]
    beside = jnp.zeros((1, 128), F32)
    for b in range(PLANES):
        moved = pltpu.roll(shared, 9 * b, 1) if b else shared
        beside = jnp.where((row >= 64 + 9 * b) & (row < 73 + 9 * b), moved[b : b + 1], beside)
    folded = [
        jnp.where(row < 64, tiles[8][0:1], turned[1:2]),
        jnp.where(row < 64, tiles[8][2:3], turned[3:4]),
        jnp.where(row < 64, tiles[8][4:5], beside),
        jnp.zeros((1, 128), F32),
    ]
    packed = jnp.concatenate([part[:PLANES] for part in parts] + folded, axis=0)
    for s in range(16):
        message[s] = packed


def fine_key(dx, dy, column, x, y):
    if dx:
        return [column - float(CX * CY - 128) if dx < 0 else column]
    if dy:
        local_y = y - float(CY - 8) if dy < 0 else y
        inside = (local_y >= 0.0) & (local_y < 8.0)
        return [jnp.where(inside, 8.0 * x + local_y, -1.0)]
    return [column, column - 256.0]


def local_kernel(bands_ref, table, g0t, g0l, g1, g2t, g2l, l1, slab, base, fine, mid):
    layer_ids = fiota((CZ, 128), 0).astype(BF16)
    mid[4:13, 32:40, :] = jnp.zeros((9, 8, CZ), F32)
    order = [(0, 0), (-1, 0), (1, 0), (0, -1), (0, 1), (-1, -1), (-1, 1), (1, -1), (1, 1)]
    for n, (dx, dy) in enumerate(order):
        spread, weights = [], []
        charge, height, column = atom_rows(table, block_index(dx, dy), 0, CAP)
        floor, above, low, high = tent_rows(charge, height)
        x, y = place_of(column)
        keys = fine_key(dx, dy, column, x, y) if (dx, dy) in FINE else []
        x = x + float(CX * dx)
        y = y + float(CY * dy)
        x0, nx_keep, nx, y0, ny = REACH[dx, dy]
        page = CZ if (dx, dy) == (0, 0) else 128
        fine_rows = page * len(keys)
        plane_x = 2.0 * (float(x0) + fiota((nx, 128), 0))
        row_y = 2.0 * (float(y0) + fiota((ny, 128), 0))
        for c in range(CAP):
            spread.append(spread_chunk(floor, above, low, high, c, layer_ids))
            column_weights = [
                jnp.where(
                    layer_ids[:page] == tall(key, c, page), jnp.ones((), BF16), jnp.zeros((), BF16)
                )
                for key in keys
            ]
            wx = hat(x[c : c + 1] - plane_x, 0.5, 0.25)
            wy = hat(y[c : c + 1] - row_y, 0.5, 0.25)
            product = (wx[:, None, :] * wy[None]).reshape(nx * ny, 128)
            weights.append(jnp.concatenate(column_weights + [product.astype(BF16)], axis=0))
        got = mm_nt(jnp.concatenate(weights, axis=1), jnp.concatenate(spread, axis=1))
        if keys:
            _, fnx, _, fny = FINE[dx, dy]
            px = {0: 4, -1: 0, 1: 20}[dx]
            py = {0: 8, -1: 0, 1: 40}[dy]
            fine[px : px + fnx, py : py + fny, :] = got[:fine_rows].reshape(fnx, fny, CZ)
        got = got[fine_rows:].reshape(nx, ny, CZ)[:nx_keep]
        new_x = {0: (0, 9), -1: (0, 4), 1: (1, 5)}[dx] if dy == 0 else (0, 0)
        if (dx, dy) == (0, -1):
            mid[4:13, 0:8, :] = got[:, :8]
            mid[4:13, 8:16, :] += got[:, 8:]
            continue
        for i in range(nx_keep):
            at = (x0 + 4 + i, slice(y0 + 8, y0 + 8 + ny))
            if new_x[0] <= i < new_x[1]:
                mid[at[0], at[1], :] = got[i]
            else:
                mid[at[0], at[1], :] += got[i]

    own = mid[4:13, 8:32, :]
    lateral = bands_ref[1, 0] * own
    for k in range(1, BANDS + 1):
        lateral += bands_ref[1, k] * (
            (mid[4 + k : 13 + k, 8:32, :] + mid[4 - k : 13 - k, 8:32, :])
            + (mid[4:13, 8 + k : 32 + k, :] + mid[4:13, 8 - k : 32 - k, :])
        )
    side_top, side_low = halves(lateral.reshape(216, CZ))
    own_top, own_low = halves(own.reshape(216, CZ))
    coarse = mm(
        jnp.concatenate([side_top, side_low, own_top, own_low, own_top], axis=1),
        jnp.concatenate([g1[...], g1[...], g2t[...], g2t[...], g2l[...]], axis=0),
    )
    coarse = jnp.concatenate([coarse, jnp.zeros((CZ - 216, CZ + 128), F32)], axis=0)
    coarse_top, coarse_low = halves(coarse)
    field_top, field_low = halves(fine[4:20, 8:40, :].reshape(CX * CY, CZ))
    total = mm(
        jnp.concatenate([l1[...], l1[...], field_top, field_low, field_top], axis=1),
        jnp.concatenate([coarse_top, coarse_low, g0t[...], g0t[...], g0l[...]], axis=0),
    )
    slab[...] = total[:, CZ:]
    for p in range(CX):
        lateral = jnp.zeros((CY, CZ), F32)
        for k in range(1, BANDS + 1):
            lateral += bands_ref[0, k] * (
                (fine[p + 4 + k, 8:40, :] + fine[p + 4 - k, 8:40, :])
                + (fine[p + 4, 8 + k : 40 + k, :] + fine[p + 4, 8 - k : 40 - k, :])
            )
        rows = slice(p * CY, (p + 1) * CY)
        base[rows, :] = total[rows, :CZ] + lateral


def circulant_kernel(gathered, cx, chunks, shared):
    top, low = halves(gathered[...].reshape(16 * MSG, 128))
    values = mm(cx[...], jnp.concatenate([top, top, low], axis=0))
    total = values[6 * CX : 7 * CX]
    for b in range(1, PLANES):
        total += pltpu.roll(values[(6 + b) * CX : (7 + b) * CX], 128 - 9 * b, 1)
    shared[...] = total
    lane = iota((CX, 128), 1)
    ninth = values[4 * CX : 5 * CX] + pltpu.roll(values[5 * CX : 6 * CX], 64, 1)
    chunks[...] = jnp.concatenate([values[: 4 * CX], jnp.where(lane < 64, ninth, 0.0)], axis=0)


def lift_kernel(where_ref, chunks, shared, base, pz, l2, partial):
    gz = where_ref[1]
    is_upper = gz == 1
    layered = mm_exact_right(chunks[...], pz[...])
    own = jnp.where(is_upper, 0.0, shared[...])
    weight = hat((iota((1, CZ), 1) - CZ).astype(F32), 1.0, 0.25)
    rows = []
    for y in range(9):
        part = layered[(y // 2) * 16 : (y // 2) * 16 + 16, (y % 2) * CZ : (y % 2 + 1) * CZ]
        rows.append(part + own[:, 64 + y : 65 + y] * weight)
    coarse = jnp.concatenate(rows, axis=0)
    partial[...] = base[...] + mm(l2[...], jnp.concatenate(halves(coarse), axis=0))


def read_kernel(where_ref, partial, across, slab, l2, table, grid, atoms):
    gz = where_ref[1]
    is_upper = gz == 1
    weight = hat((iota((1, 128), 1) - 128 * (1 - gz)).astype(F32), 1.0, 0.25)
    rows = [across[:, 64 + y : 65 + y] * weight for y in range(9)]
    near = slab[...] + mm(l2[...], jnp.concatenate(halves(jnp.concatenate(rows, axis=0)), axis=0))
    low = jnp.where(is_upper, near, 0.0)
    high = jnp.where(is_upper, 0.0, near)
    potential = partial[...] + jnp.concatenate([low, high], axis=1)
    grid[...] = potential.reshape(CX, CY, CZ)
    turned = potential.T.astype(BF16)
    _, height, column = atom_rows(table, OWN, 0, CAP)
    layer_ids = fiota((CZ, 128), 0)
    row_ids = layer_ids.astype(BF16)
    keys = fine_key(0, 0, column, None, None)
    for c in range(0, CAP, 2):
        one = [
            jnp.concatenate(
                [
                    jnp.where(row_ids == tall(key, d, CZ), jnp.ones((), BF16), jnp.zeros((), BF16))
                    for key in keys
                ],
                axis=0,
            )
            for d in (c, c + 1)
        ]
        read = mm(turned, jnp.concatenate(one, axis=1))
        for i, d in enumerate((c, c + 1)):
            tent = jnp.maximum(0.0, 1.0 - jnp.abs(layer_ids - height[d : d + 1]))
            atoms[d : d + 1, :] = jnp.sum(
                read[:, i * 128 : (i + 1) * 128] * tent, axis=0, keepdims=True
            )


def vmem():
    return pl.BlockSpec(memory_space=pltpu.VMEM)


def smem():
    return pl.BlockSpec(memory_space=pltpu.SMEM)


def shaped(*pairs):
    return tuple(jax.ShapeDtypeStruct(shape, dtype) for shape, dtype in pairs)


PARAMS = pltpu.CompilerParams(vmem_limit_bytes=VMEM_LIMIT)


def local(charges, heights, columns, counts, bands, cycle_kernel):
    place = jnp.stack([lax.axis_index("gx"), lax.axis_index("gz")]).astype(jnp.int32)
    sent = pl.pallas_call(
        pack_kernel,
        in_specs=[pl.BlockSpec(memory_space=pltpu.HBM)] * 4,
        out_specs=vmem(),
        out_shape=jax.ShapeDtypeStruct((SENDERS, 1, FIELDS), F32),
        scratch_shapes=[
            pltpu.VMEM((CAP, SENDERS), F32),
            pltpu.VMEM((CAP, SENDERS), F32),
            pltpu.VMEM((CAP, SENDERS), jnp.int32),
            pltpu.VMEM((1, SENDERS), jnp.int32),
            pltpu.SemaphoreType.DMA((4,)),
        ],
        name="pack",
    )(charges[0, 0].T, heights[0, 0].T, columns[0, 0].T, counts[0])
    arrived = lax.all_to_all(sent, ("gx", "gy"), split_axis=0, concat_axis=0, tiled=True)
    wide = CZ + 128
    g0t, g0l, g1, g2t, g2l, l1, l2, cx, pz = pl.pallas_call(
        tables_kernel,
        in_specs=[smem(), smem(), smem()],
        out_specs=[vmem()] * 9,
        out_shape=shaped(
            ((CZ, wide), BF16),
            ((CZ, wide), BF16),
            ((CZ, wide), BF16),
            ((CZ, wide), BF16),
            ((CZ, wide), BF16),
            ((CX * CY, CZ), BF16),
            ((CX * CY, 2 * 9 * CX), BF16),
            ((TABLE_ROWS, 3 * 16 * MSG), BF16),
            ((128, 2 * CZ), BF16),
        ),
        compiler_params=PARAMS,
        name="tables",
    )(place, bands, cycle_kernel)
    arrived, g0t, g0l, g1, g2t, g2l, l1, l2, cx, pz = lax.optimization_barrier(
        (arrived, g0t, g0l, g1, g2t, g2l, l1, l2, cx, pz)
    )
    table, message = pl.pallas_call(
        coarse_kernel,
        in_specs=[smem(), vmem()],
        out_specs=[vmem()] * 2,
        out_shape=shaped(((FIELDS, 128), F32), ((16, MSG, 128), F32)),
        compiler_params=PARAMS,
        name="coarse",
    )(place, arrived)
    gathered = lax.all_to_all(message, "gx", split_axis=0, concat_axis=0, tiled=True)
    slab, base = pl.pallas_call(
        local_kernel,
        in_specs=[smem()] + [vmem()] * 7,
        out_specs=[vmem()] * 2,
        out_shape=shaped(((CX * CY, 128), F32), ((CX * CY, CZ), F32)),
        scratch_shapes=[
            pltpu.VMEM((CX + 2 * BANDS, CY + 16, CZ), F32),
            pltpu.VMEM((17, 40, CZ), F32),
        ],
        compiler_params=PARAMS,
        name="local",
    )(bands, table, g0t, g0l, g1, g2t, g2l, l1)
    gathered, slab, base = lax.optimization_barrier((gathered, slab, base))
    slab = lax.ppermute(slab, "gz", [(0, 1), (1, 0)])
    chunks, shared = pl.pallas_call(
        circulant_kernel,
        in_specs=[vmem()] * 2,
        out_specs=[vmem()] * 2,
        out_shape=shaped(((5 * CX, 128), F32), ((CX, 128), F32)),
        compiler_params=PARAMS,
        name="circulant",
    )(gathered, cx)
    across = lax.ppermute(shared, "gz", [(0, 1), (1, 0)])
    partial = pl.pallas_call(
        lift_kernel,
        in_specs=[smem()] + [vmem()] * 5,
        out_specs=vmem(),
        out_shape=jax.ShapeDtypeStruct((CX * CY, CZ), F32),
        compiler_params=PARAMS,
        cost_estimate=pl.CostEstimate(flops=10**9, bytes_accessed=4 * 10**6, transcendentals=0),
        name="lift",
    )(place, chunks, shared, base, pz, l2)
    grid, atoms = pl.pallas_call(
        read_kernel,
        in_specs=[smem()] + [vmem()] * 5,
        out_specs=[vmem()] * 2,
        out_shape=shaped(((CX, CY, CZ), F32), ((CAP, SENDERS), F32)),
        compiler_params=PARAMS,
        name="read",
    )(place, partial, across, slab, l2, table)
    return grid, atoms.T[None, None]


def solution(mesh):
    placed = (
        P("gz", ("gx", "gy"), None, None),
        P("gz", ("gx", "gy"), None, None),
        P("gz", ("gx", "gy"), None, None),
        P("gz", ("gx", "gy"), None),
        P(),
        P(),
    )
    return jax.shard_map(
        local,
        mesh=mesh,
        in_specs=placed,
        out_specs=(P("gx", "gy", "gz"), P("gz", ("gx", "gy"), None, None)),
        check_vma=False,
    )
```
